256 devices in a mesh: band: 8 (over y, core), fft: 32 (over x, z).
Axes of the slice: x: 4, y: 4, z: 8, core: 2. Of those that a mesh axis runs over, the one named last changes fastest.
Arguments:
- psi: bfloat16 [16, 2, 2560, 128], P('band', None, 'fft'), may hold values from -6 to 6
- stick_col: int32 [2560], replicated, may hold values from 0 to 15420, as said below
- stick_len: int32 [2560], replicated, may hold values from 0 to 121, as said below
- plane_z: int32 [256], replicated, may hold values from -1 to 239, as said below
- potential: float32 [256, 57600], P('fft'), may hold values from -12 to 12
- beta: bfloat16 [8, 8, 2, 2560, 128], P('band', None, None, 'fft'), may hold values from -0.01953125 to 0.01953125
- coupling: float32 [8, 8, 8], replicated, may hold values from -80 to 80
Outputs:
- hpsi: float32 [16, 2, 2560, 128], P('band', None, 'fft')
The draws below stay inside these ranges and needn't reach their ends.
Inputs may be any that keep to these rules, and one draw needn't show every extreme that they name: stick_col[i] = (gx + 60) * 128 + gy + 60 for the stick in slot i, where slots i = d * 80 .. (d + 1) * 80 - 1 belong to index d of fft and the used ones come first; every used stick has gx^2 + gy^2 <= 60^2 and no column is used twice; empty slots hold 0. stick_len[i] = 2 h + 1 with h the largest integer such that gx^2 + gy^2 + h^2 <= 60^2, for used slots, and 0 for empty ones; an index of fft holds at most 80 sticks, one holds exactly 80, and all together hold 1280. Slot t of index d of fft is plane_z[d * 8 + t], or -1 when empty; used slots come first and hold consecutive planes, every plane 0 .. 239 is held once, and the numbers of planes held by two indices differ by at most one.
All inputs are finite; a program needn't handle non-finite values.
Results may differ from the reference program's by a relative error of at most 0.015.
Values may be sent and summed in bfloat16 or wider, within the bound.
A program may use at most 64 MiB of HBM per device.

```python
import math
import jax
import jax.numpy as jnp
import numpy as np
from jax import lax

NG = 240
RAD = 60
STICK_WIDTH = 128
STICK_MEAN = 40
SLOTS = 80
TOTAL_SLOTS = 2560
NSTICK = 1280
PLANES = 8
NZS = 256
BAND_COUNT = 16
ATOM_DEV = 1
ATOM_PROJECTORS = 8
ATOM_COUNT = 8
N_BAND = 8
N_FFT = 32


def circle_columns():
    radius = NG // 4
    stick_span = 2 * radius + 8
    leading = [(0, 0), (radius, 0)]
    others = [(wave_x, wave_y) for wave_x in range(-radius, radius + 1) for wave_y in range(-radius, radius + 1) if wave_x * wave_x + wave_y * wave_y <= radius * radius and (wave_x, wave_y) not in leading]
    columns = leading + others
    table_col = np.array([(wave_x + radius) * stick_span + wave_y + radius for wave_x, wave_y in columns], np.int32)
    table_len = np.array([2 * math.isqrt(radius * radius - wave_x * wave_x - wave_y * wave_y) + 1 for wave_x, wave_y in columns], np.int32)
    return (table_col, table_len)


def stick_tables(key):
    table_col, table_len = circle_columns()
    circle_size = table_col.shape[0]
    shuffled = jax.random.permutation(jax.random.fold_in(key, 1), circle_size - 2).astype(jnp.int32) + 2
    stick_order = jnp.concatenate([jnp.arange(2, dtype=jnp.int32), shuffled])[:NSTICK]
    devices_order = jax.random.permutation(jax.random.fold_in(key, 2), N_FFT).astype(jnp.int32)
    shifts = jax.random.randint(jax.random.fold_in(key, 3), (N_FFT // 2,), 0, STICK_MEAN + 1).astype(jnp.int32)
    shifts = shifts.at[0].set(STICK_MEAN)
    counts = jnp.zeros((N_FFT,), jnp.int32).at[devices_order[0::2]].set(STICK_MEAN + shifts)
    counts = counts.at[devices_order[1::2]].set(STICK_MEAN - shifts)
    starts = jnp.cumsum(counts) - counts
    stick_slot_index = jnp.arange(TOTAL_SLOTS, dtype=jnp.int32)
    owner_dev = stick_slot_index // SLOTS
    within = stick_slot_index % SLOTS
    in_use = within < counts[owner_dev]
    stick_pick = jnp.clip(starts[owner_dev] + within, 0, NSTICK - 1)
    stick_id = stick_order[stick_pick]
    stick_col = jnp.where(in_use, jnp.asarray(table_col)[stick_id], 0).astype(jnp.int32)
    stick_len = jnp.where(in_use, jnp.asarray(table_len)[stick_id], 0).astype(jnp.int32)
    return (stick_col, stick_len)


def draw_stick_col(key, part):
    tables = stick_tables(key)
    return tables[0]


def draw_stick_len(key, part):
    tables = stick_tables(key)
    return tables[1]


def draw_plane_z(key, part):
    key = jax.random.fold_in(key, 7)
    devices_order = jax.random.permutation(key, N_FFT).astype(jnp.int32)
    ranks = jnp.argsort(devices_order).astype(jnp.int32)
    counts = NG // N_FFT + (ranks < NG % N_FFT).astype(jnp.int32)
    starts = ranks * (NG // N_FFT) + jnp.minimum(ranks, NG % N_FFT)
    stick_slot_index = jnp.arange(NZS, dtype=jnp.int32)
    owner_dev = stick_slot_index // PLANES
    within = stick_slot_index % PLANES
    return jnp.where(within < counts[owner_dev], starts[owner_dev] + within, -1).astype(jnp.int32)


def block_scale(rng, extent, split, smallest, high):
    def one(dim, parts):
        heights = jax.random.uniform(jax.random.fold_in(jax.random.fold_in(rng, 6), dim), (parts,), jnp.float32, smallest / len(split), high / len(split))
        return jnp.repeat(jnp.exp(heights), extent[dim] // parts).reshape((-1,) + (1,) * (len(extent) - dim - 1))

    gain = one(*split[0])
    for cut in split[1:]:
        gain = gain * one(*cut)
    return gain


def bell_draw(stream_key, dims, width, reach, pieces=(), kind=jnp.bfloat16):
    gain = block_scale(stream_key, dims, pieces, -0.22, 0.18) if pieces else 1.0
    result = jax.random.normal(stream_key, dims, jnp.float32) * width * gain
    return jnp.minimum(jnp.maximum(result, -reach), reach).astype(kind)


def setup_inputs(seed: int = 0) -> dict:
    arg_keys = jax.random.split(jax.random.key(seed), 8)
    psi = bell_draw(arg_keys[0], (BAND_COUNT, 2, TOTAL_SLOTS, STICK_WIDTH), 1.0, 6.0, ((0, 8), (2, 32)))
    stick_col = draw_stick_col(jax.random.fold_in(arg_keys[7], 71), 0)
    stick_len = draw_stick_len(jax.random.fold_in(arg_keys[7], 71), 0)
    plane_z = draw_plane_z(jax.random.fold_in(arg_keys[7], 71), 0)
    potential = bell_draw(arg_keys[4], (NZS, NG * NG), 2.0, 12.0, ((0, 32),), jnp.float32)
    beta = bell_draw(arg_keys[5], (ATOM_COUNT, ATOM_PROJECTORS, 2, TOTAL_SLOTS, STICK_WIDTH), (TOTAL_SLOTS * STICK_WIDTH // 3) ** -0.5, 0.01953125, ((0, 8), (3, 32)))
    coupling = bell_draw(arg_keys[6], (ATOM_COUNT, ATOM_PROJECTORS, ATOM_PROJECTORS), (0.3 * (TOTAL_SLOTS * STICK_WIDTH // (3 * ATOM_COUNT * ATOM_PROJECTORS)) ** 0.5), 80.0, (), jnp.float32)
    return dict(psi=psi, stick_col=stick_col, stick_len=stick_len, plane_z=plane_z, potential=potential, beta=beta, coupling=coupling)


def sphere_mask(stick_len, stick_span, radius):
    offset = jnp.abs(jnp.arange(stick_span, dtype=jnp.int32) - radius)
    return (2 * offset[None, :] < stick_len[:, None]).astype(jnp.float32)


def kinetic_table(stick_col, stick_span, radius):
    wave_x = stick_col // stick_span - radius
    wave_y = stick_col % stick_span - radius
    wave_z = jnp.arange(stick_span, dtype=jnp.int32) - radius
    square = (wave_x * wave_x + wave_y * wave_y)[:, None] + (wave_z * wave_z)[None, :]
    return square.astype(jnp.float32) / float(radius * radius)


def einsum_high(pattern, left_side, right_side):
    return jnp.einsum(pattern, left_side, right_side, precision=lax.Precision.HIGHEST)


def projections(beta_part, waves):
    real_out = einsum_high("akst,bst->akb", beta_part[:, :, 0], waves[:, 0]) + einsum_high("akst,bst->akb", beta_part[:, :, 1], waves[:, 1])
    imag_out = einsum_high("akst,bst->akb", beta_part[:, :, 0], waves[:, 1]) - einsum_high("akst,bst->akb", beta_part[:, :, 1], waves[:, 0])
    return jnp.stack([real_out, imag_out])


def apply_projectors(beta_part, coeffs):
    real_out = einsum_high("akst,akb->bst", beta_part[:, :, 0], coeffs[0]) - einsum_high("akst,akb->bst", beta_part[:, :, 1], coeffs[1])
    imag_out = einsum_high("akst,akb->bst", beta_part[:, :, 0], coeffs[1]) + einsum_high("akst,akb->bst", beta_part[:, :, 1], coeffs[0])
    return jnp.stack([real_out, imag_out], axis=1)


def reference(psi, stick_col, stick_len, plane_z, potential, beta, coupling):
    in_sphere = sphere_mask(stick_len, STICK_WIDTH, RAD)
    waves = psi.astype(jnp.float32) * in_sphere
    kinetic = kinetic_table(stick_col, STICK_WIDTH, RAD)

    nonlocal_sum = jnp.zeros(waves.shape, jnp.float32)
    for group_index in range(N_BAND):
        low_atom = group_index * ATOM_DEV
        beta_part = beta[low_atom:low_atom + ATOM_DEV].astype(jnp.float32) * in_sphere
        projected = projections(beta_part, waves)
        coeffs = einsum_high("akj,cajb->cakb", coupling[low_atom:low_atom + ATOM_DEV], projected).astype(jnp.bfloat16)
        group_term = apply_projectors(beta_part, coeffs.astype(jnp.float32))
        nonlocal_sum = nonlocal_sum + lax.optimization_barrier(group_term.astype(jnp.bfloat16)).astype(jnp.float32)

    index_x = (stick_col // STICK_WIDTH - RAD) % NG
    index_y = (stick_col % STICK_WIDTH - RAD) % NG
    index_z = (jnp.arange(STICK_WIDTH, dtype=jnp.int32) - RAD) % NG
    plane_safe = jnp.where(plane_z >= 0, plane_z, NG)
    potential_grid = jnp.zeros((NG, NG * NG), jnp.float32).at[plane_safe].set(potential, mode="drop").reshape(NG, NG, NG)

    def one_band(wave_field):
        grid_real = jnp.zeros((NG, NG, NG), jnp.float32).at[index_z[None, :], index_x[:, None], index_y[:, None]].add(wave_field[0])
        grid_imag = jnp.zeros((NG, NG, NG), jnp.float32).at[index_z[None, :], index_x[:, None], index_y[:, None]].add(wave_field[1])
        values = jnp.fft.ifftn(grid_real + 1j * grid_imag) * float(NG ** 3)
        weighted = potential_grid * values
        returned = jnp.fft.fftn(weighted) / float(NG ** 3)
        picked = returned[index_z[None, :], index_x[:, None], index_y[:, None]]
        return jnp.stack([jnp.real(picked), jnp.imag(picked)])

    local_term = lax.map(one_band, waves)
    return in_sphere * (kinetic * waves + local_term + nonlocal_sum)
```

```python
import functools
import math

import jax
import jax.numpy as jnp
import numpy as np
from jax import lax
from jax.experimental import pallas as pl
from jax.experimental.pallas import tpu as pltpu
from jax.sharding import PartitionSpec as P

NG = 240
RAD = 60
W = 128
SLOTS = 80
PLANES = 8
LOW = 16
F32 = jnp.float32
BF16 = jnp.bfloat16
MESH = pl.DeviceIdType.MESH


def tables():
    wave = np.arange(W) - RAD
    pos = np.arange(256)
    angle = 2.0 * np.pi * ((wave[:, None] * pos[None, :]) % NG) / NG
    inside = (pos < NG)[None, :]
    co, si = np.cos(angle) * inside, np.sin(angle) * inside
    z_re = np.concatenate([co.T, -si.T], axis=1)
    z_im = np.concatenate([si.T, co.T], axis=1)
    y_out = np.block([[co, si], [-si, co]])
    y_back = y_out.T
    cx, sx = co[:, :NG].T, si[:, :NG].T
    x_out = np.block([[cx, -sx], [sx, cx]])
    x_back = x_out.T
    return [np.asarray(t, np.float32).astype(jnp.bfloat16) for t in (np.stack([z_re, z_im]), y_out, x_out, x_back, y_back)]


def iota(shape, dim):
    return lax.broadcasted_iota(jnp.int32, shape, dim)


def dot(a, b, dims=((1,), (0,)), precision=None):
    return lax.dot_general(a, b, (dims, ((), ())), preferred_element_type=F32, precision=precision)


NT = ((1,), (1,))
TN = ((0,), (0,))


def kernel(
    n_band, n_fft,
    len_s, col_s, plane_ref, col_ref, psi_ref, pot_ref, beta_ref, coup_ref,
    zt_ref, yf_ref, xf_ref, xb_ref, yb_ref,
    out_ref,
    lenb, colb, psi2, z_tab, send1, recv1, send2, recv2,
    xhot, yhot, v3, dense, lhs, yin, boxb,
    gath, beta_f, beta_t, psi_f, psi_t, part_send, part_recv, term_f, term_send, term_recv,
    s1, r1, s2, r2, sg, rg, sp, rp, sn, rn,
):
    f = lax.axis_index("fft")
    g = lax.axis_index("band")
    nb = 2
    tot = n_fft * SLOTS
    nq = 2 * PLANES
    groups = n_fft // 8

    barrier = pltpu.get_barrier_semaphore()

    @pl.loop(1, n_fft)
    def _(k):
        pl.semaphore_signal(barrier, inc=1, device_id={"fft": lax.rem(f + k, n_fft)}, device_id_type=MESH)

    @pl.loop(1, n_band)
    def _(k):
        pl.semaphore_signal(barrier, inc=1, device_id={"band": lax.rem(g + k, n_band)}, device_id_type=MESH)

    @pl.loop(0, SLOTS)
    def _(s):
        lenb[pl.ds(s, 1), :] = jnp.full((1, W), len_s[f * SLOTS + s], jnp.int32)
        colb[pl.ds(s, 1), :] = jnp.full((1, W), col_s[f * SLOTS + s], jnp.int32)

    wave_z = iota((SLOTS, W), 1) - RAD
    in_sphere = (2 * jnp.abs(wave_z) < lenb[...]).astype(F32)
    psi2[...] = jnp.zeros(psi2.shape, BF16)
    for b in range(nb):
        for c in range(2):
            psi2[b, 0:SLOTS, c * W:(c + 1) * W] = (psi_ref[b, c].astype(F32) * in_sphere).astype(BF16)

    n_slot = n_fft * PLANES
    hot_z = (iota((256, n_slot), 0) == plane_ref[...]).astype(F32).T.astype(BF16)
    z_re = dot(hot_z, zt_ref[0]).reshape(n_fft, 1, PLANES, 256)
    z_im = dot(hot_z, zt_ref[1]).reshape(n_fft, 1, PLANES, 256)
    z_tab[...] = jnp.concatenate([z_re, z_im], axis=1).reshape(n_fft * nq, 256).astype(BF16)
    for b in range(nb):
        along = dot(z_tab[...], psi2[b], NT)
        send1[b] = along.reshape(n_fft, nq, W).astype(BF16)
        recv1[b, f] = send1[b, f]

    pl.semaphore_wait(barrier, n_fft + n_band - 2)

    def exchange(send, recv, send_sem, recv_sem, b):
        @pl.loop(1, n_fft)
        def _(k):
            e = lax.rem(f + k, n_fft)
            pltpu.make_async_remote_copy(
                src_ref=send.at[b, e], dst_ref=recv.at[b, f], send_sem=send_sem.at[b], recv_sem=recv_sem.at[b],
                device_id={"fft": e}, device_id_type=MESH,
            ).start()

    def wait_bytes(ref, sem):
        pltpu.make_async_copy(ref, ref, sem).wait()

    exchange(send1, recv1, s1, r1, 0)

    @pl.loop(1, n_band)
    def _(k):
        pltpu.make_async_remote_copy(
            src_ref=psi_ref, dst_ref=gath.at[g], send_sem=sg, recv_sem=rg,
            device_id={"band": lax.rem(g + k, n_band)}, device_id_type=MESH,
        ).start()

    exchange(send1, recv1, s1, r1, 1)
    gath[g] = psi_ref[...]

    for r in range(tot // W):
        col = col_ref[r:r + 1, :]
        c, d = col // W, col % W
        low, high = c % LOW, (c // LOW) * W + d
        xhot[:, r * W:(r + 1) * W] = (iota((LOW, W), 0) == low).astype(F32).astype(BF16)
        for m in range(2):
            yhot[m * 512:(m + 1) * 512, r * W:(r + 1) * W] = (iota((512, W), 0) + m * 512 == high).astype(F32).astype(BF16)

    @pl.loop(0, NG // 8)
    def _(m):
        for r in range(8):
            start = 240 * r
            low = start // W * W
            width = 256 if start - low <= 16 else 384
            piece = pot_ref[:, pl.ds(pl.multiple_of(m * 1920 + low, W), width)]
            if start - low:
                piece = pltpu.roll(piece, width - (start - low), 1)
            for c in range(2):
                v3[c, pl.ds(pl.multiple_of((m * 8 + r) * 8, 8), 8), :] = piece[:, c * W:(c + 1) * W]

    for k in range(8):
        for c in range(2):
            beta_f[pl.ds((k * 2 + c) * SLOTS, SLOTS), :] = beta_ref[0, k, c].astype(F32) * in_sphere

    @pl.loop(0, SLOTS)
    def _(s):
        rows = [beta_f[pl.ds(c * SLOTS + s, 8, stride=2 * SLOTS), :] for c in range(2)]
        beta_t[:, pl.ds(pl.multiple_of(s * W, W), W)] = jnp.concatenate(rows, axis=0).astype(BF16)

    spread = (iota((nq * LOW, nq), 0) // LOW == iota((nq * LOW, nq), 1)).astype(F32).astype(BF16)
    gather = (iota((nq, nq * LOW), 1) // LOW == iota((nq, nq * LOW), 0)).astype(F32).astype(BF16)
    lane16 = iota((nq, W), 1)

    def to_planes(b):
        wait_bytes(recv1.at[b, pl.ds(0, n_fft - 1)], r1.at[b])

        @pl.loop(0, groups)
        def _(h):
            outs = [jnp.zeros((nq, W), F32)] * 5
            for i in range(8):
                piece = recv1[b, h * 8 + i].astype(F32)
                off = 80 * i % W
                first = 80 * i // W
                rolled = pltpu.roll(piece, off, 1) if off else piece
                top = min(off + 80, W)
                outs[first] = jnp.where((lane16 >= off) & (lane16 < top), rolled, outs[first])
                if off + 80 > W:
                    outs[first + 1] = jnp.where(lane16 < off + 80 - W, rolled, outs[first + 1])
            at = pl.ds(pl.multiple_of(h * 640, W), 640)
            piece = jnp.concatenate(outs, axis=1).astype(BF16)
            dense[:, at] = piece
            repeated = dot(spread, piece).astype(BF16).reshape(nq, LOW, 640)
            lhs[:, at] = (repeated * xhot[:, at][None]).reshape(nq * LOW, 640)

        @pl.loop(0, 4)
        def _(n):
            placed = dot(lhs[...], yhot[pl.ds(pl.multiple_of(n * 256, 256), 256), :], NT).astype(BF16)
            placed = placed.reshape(2, PLANES, LOW, 256)
            for h in range(2):
                for c in range(2):
                    yin[:, pl.ds(pl.multiple_of((n * 2 + h) * LOW, LOW), LOW), c * W:(c + 1) * W] = placed[c, :, :, h * W:(h + 1) * W]

        @pl.loop(0, PLANES // 2)
        def _(pair):
            for u in range(2):
                t = pair * 2 + u
                half = dot(yin[t], yf_ref[...]).astype(BF16)
                half = jnp.concatenate([half[:, :256], half[:, 256:]], axis=0)
                full = dot(xf_ref[...], half).reshape(2, NG, 256)
                weight = jnp.concatenate([v3[c, pl.ds(t, NG, stride=PLANES), :] for c in range(2)], axis=1)
                weighted = (full * weight[None]).astype(BF16).reshape(2 * NG, 256)
                back = dot(xb_ref[...], weighted).astype(BF16)
                back = jnp.concatenate([back[:W], back[W:]], axis=1)
                box = dot(back, yb_ref[...]).astype(BF16)
                for c in range(2):
                    for h in range(W // LOW):
                        boxb[c, t, :, h * W:(h + 1) * W] = box[h * LOW:(h + 1) * LOW, c * W:(c + 1) * W]

    def to_sticks(b):
        boxes = boxb[...].reshape(nq * LOW, 1024)

        @pl.loop(0, tot // 640)
        def _(h):
            at = pl.ds(pl.multiple_of(h * 640, W), 640)
            rows = dot(boxes, yhot[:, at]).astype(BF16).reshape(nq, LOW, 640) * xhot[:, at][None]
            picked = dot(gather, rows.reshape(nq * LOW, 640))
            for i in range(8):
                off = 80 * i % W
                first = 80 * i // W
                piece = picked[:, first * W:(first + 1) * W]
                if off:
                    piece = pltpu.roll(piece, W - off, 1)
                if off + 80 > W:
                    other = pltpu.roll(picked[:, (first + 1) * W:(first + 2) * W], W - off, 1)
                    piece = jnp.where(lane16 < W - off, piece, other)
                send2[b, h * 8 + i] = jnp.where(lane16 < 80, piece, 0.0).astype(BF16)

        recv2[b, f] = send2[b, f]
        exchange(send2, recv2, s2, r2, b)

    nbr = 2 * nb * n_band
    swap = (
        ((iota((nbr, nbr), 0) == iota((nbr, nbr), 1) + 1) & (iota((nbr, nbr), 0) % 2 == 1)).astype(F32)
        - ((iota((nbr, nbr), 0) + 1 == iota((nbr, nbr), 1)) & (iota((nbr, nbr), 0) % 2 == 0)).astype(F32)
    )

    def project():
        wait_bytes(gath.at[pl.ds(0, n_band - 1)], rg)
        for h in range(n_band):
            psi_f[pl.ds(h * 4 * SLOTS, 4 * SLOTS), :] = gath[h].reshape(4 * SLOTS, W).astype(F32)

        @pl.loop(0, SLOTS)
        def _(s):
            psi_t[:, pl.ds(pl.multiple_of(s * W, W), W)] = psi_f[pl.ds(s, nbr, stride=SLOTS), :].astype(BF16)

        prod = dot(beta_t[...], psi_t[...], NT)
        part = prod[:8] + dot(prod[8:], swap, precision=lax.Precision.HIGHEST)
        part_send[...] = jnp.zeros((8, W), F32)
        part_send[:, :nbr] = part
        part_recv[f] = part_send[...]

        @pl.loop(1, n_fft)
        def _(k):
            pltpu.make_async_remote_copy(
                src_ref=part_send, dst_ref=part_recv.at[f], send_sem=sp, recv_sem=rp,
                device_id={"fft": lax.rem(f + k, n_fft)}, device_id_type=MESH,
            ).start()

    def expand():
        wait_bytes(part_recv.at[pl.ds(0, n_fft - 1)], rp)
        whole = jnp.sum(part_recv[...], axis=0)[:, :nbr]
        coeffs = dot(coup_ref[g], whole, precision=lax.Precision.HIGHEST).astype(BF16).astype(F32)
        crossed = dot(coeffs, swap, precision=lax.Precision.HIGHEST)
        factors = jnp.concatenate([coeffs, -crossed], axis=0).astype(BF16)

        @pl.loop(0, SLOTS // 8)
        def _(m):
            terms = dot(factors, beta_t[:, pl.ds(pl.multiple_of(m * 1024, 1024), 1024)], TN)
            for i in range(8):
                term_f[pl.ds(m * 8 + i, nbr, stride=SLOTS), :] = terms[:, i * W:(i + 1) * W]

        for h in range(n_band):
            term_send[h] = term_f[pl.ds(h * 4 * SLOTS, 4 * SLOTS), :].astype(BF16)
        term_recv[g] = term_send[g]

        @pl.loop(1, n_band)
        def _(k):
            e = lax.rem(g + k, n_band)
            pltpu.make_async_remote_copy(
                src_ref=term_send.at[e], dst_ref=term_recv.at[g], send_sem=sn, recv_sem=rn,
                device_id={"band": e}, device_id_type=MESH,
            ).start()

    to_planes(0)
    project()
    to_sticks(0)
    to_planes(1)
    expand()
    to_sticks(1)

    gx, gy = colb[...] // W - RAD, colb[...] % W - RAD
    kinetic = (gx * gx + gy * gy + wave_z * wave_z).astype(F32) / float(RAD * RAD)
    wait_bytes(term_recv.at[pl.ds(0, n_band - 1)], rn)
    for b in range(nb):
        wait_bytes(recv2.at[b, pl.ds(0, n_fft - 1)], r2.at[b])
        local = dot(recv2[b].reshape(n_fft * nq, W), z_tab[...], TN) * (1.0 / float(NG**3))
        for c in range(2):
            at = pl.ds((b * 2 + c) * SLOTS, SLOTS)
            nonlocal_sum = term_recv[0, at, :].astype(F32)
            for h in range(1, n_band):
                nonlocal_sum = nonlocal_sum + term_recv[h, at, :].astype(F32)
            wave = psi_ref[b, c].astype(F32) * in_sphere
            out_ref[b, c] = in_sphere * (kinetic * wave + local[:SLOTS, c * W:(c + 1) * W] + nonlocal_sum)

    for b in range(nb):
        wait_bytes(send1.at[b, pl.ds(0, n_fft - 1)], s1.at[b])
        wait_bytes(send2.at[b, pl.ds(0, n_fft - 1)], s2.at[b])
    wait_bytes(gath.at[pl.ds(0, n_band - 1)], sg)
    wait_bytes(part_recv.at[pl.ds(0, n_fft - 1)], sp)
    wait_bytes(term_send.at[pl.ds(0, n_band - 1)], sn)


def body(n_band, n_fft, psi, stick_col, stick_len, plane_z, potential, beta, coupling):
    tot = n_fft * SLOTS
    n_slot = n_fft * PLANES
    nq = 2 * PLANES
    nbr = 4 * n_band
    consts = [jnp.asarray(t) for t in tables()]
    vmem = pl.BlockSpec(memory_space=pltpu.VMEM)
    smem = pl.BlockSpec(memory_space=pltpu.SMEM)
    dma = pltpu.SemaphoreType.DMA
    return pl.pallas_call(
        functools.partial(kernel, n_band, n_fft),
        out_shape=jax.ShapeDtypeStruct(psi.shape, F32),
        in_specs=[smem, smem] + [vmem] * 11,
        out_specs=vmem,
        scratch_shapes=[
            pltpu.VMEM((SLOTS, W), jnp.int32),
            pltpu.VMEM((SLOTS, W), jnp.int32),
            pltpu.VMEM((2, W, 2 * W), BF16),
            pltpu.VMEM((n_fft * nq, 2 * W), BF16),
            pltpu.VMEM((2, n_fft, nq, W), BF16),
            pltpu.VMEM((2, n_fft, nq, W), BF16),
            pltpu.VMEM((2, n_fft, nq, W), BF16),
            pltpu.VMEM((2, n_fft, nq, W), BF16),
            pltpu.VMEM((LOW, tot), BF16),
            pltpu.VMEM((1024, tot), BF16),
            pltpu.VMEM((2, NG * PLANES, W), F32),
            pltpu.VMEM((nq, tot), BF16),
            pltpu.VMEM((nq * LOW, tot), BF16),
            pltpu.VMEM((PLANES, W, 2 * W), BF16),
            pltpu.VMEM((2, PLANES, LOW, 1024), BF16),
            pltpu.VMEM((n_band, 2, 2, SLOTS, W), BF16),
            pltpu.VMEM((16 * SLOTS, W), F32),
            pltpu.VMEM((16, SLOTS * W), BF16),
            pltpu.VMEM((nbr * SLOTS, W), F32),
            pltpu.VMEM((nbr, SLOTS * W), BF16),
            pltpu.VMEM((8, W), F32),
            pltpu.VMEM((n_fft, 8, W), F32),
            pltpu.VMEM((nbr * SLOTS, W), F32),
            pltpu.VMEM((n_band, 4 * SLOTS, W), BF16),
            pltpu.VMEM((n_band, 4 * SLOTS, W), BF16),
            dma((2,)), dma((2,)), dma((2,)), dma((2,)),
            dma, dma, dma, dma, dma, dma,
        ],
        compiler_params=pltpu.CompilerParams(
            collective_id=0, has_side_effects=True, vmem_limit_bytes=56 * 1024 * 1024
        ),
    )(
        stick_len, stick_col, plane_z.reshape(1, n_slot), stick_col.reshape(tot // W, W),
        psi, potential, beta, coupling, *consts,
    )


def solution(mesh):
    in_specs = (
        P("band", None, "fft", None),
        P(),
        P(),
        P(),
        P("fft", None),
        P("band", None, None, "fft", None),
        P(),
    )
    out_specs = P("band", None, "fft", None)
    part = functools.partial(body, mesh.shape["band"], mesh.shape["fft"])
    return jax.shard_map(part, mesh=mesh, in_specs=in_specs, out_specs=out_specs, check_vma=False)
```

```python
import functools
import math

import jax
import jax.numpy as jnp
import numpy as np
from jax import lax
from jax.experimental import pallas as pl
from jax.experimental.pallas import tpu as pltpu
from jax.sharding import PartitionSpec as P

NG = 240
RAD = 60
W = 128
SLOTS = 80
PLANES = 8
LOW = 64
PAD = 88
F32 = jnp.float32
BF16 = jnp.bfloat16
MESH = pl.DeviceIdType.MESH


def tables():
    wave = np.arange(W) - RAD
    pos = np.arange(256)
    angle = 2.0 * np.pi * ((wave[:, None] * pos[None, :]) % NG) / NG
    inside = (pos < NG)[None, :]
    co, si = np.cos(angle) * inside, np.sin(angle) * inside
    z_re = np.concatenate([co.T, -si.T], axis=1)
    z_im = np.concatenate([si.T, co.T], axis=1)
    y_out = np.block([[co, si], [-si, co]])
    y_back = y_out.T
    cx, sx = co[:, :NG].T, si[:, :NG].T
    x_out = np.block([[cx, -sx], [sx, cx]])
    x_out = x_out.reshape(2 * NG, 2, W).transpose(0, 2, 1).reshape(2 * NG, 2 * W)
    x_back = x_out.T
    return [np.asarray(t, np.float32).astype(jnp.bfloat16) for t in (np.stack([z_re, z_im]), y_out, x_out, x_back, y_back)]


def iota(shape, dim):
    return lax.broadcasted_iota(jnp.int32, shape, dim)


def dot(a, b, dims=((1,), (0,)), precision=None):
    return lax.dot_general(a, b, (dims, ((), ())), preferred_element_type=F32, precision=precision)


NT = ((1,), (1,))
TN = ((0,), (0,))


def kernel(
    n_band, n_fft,
    len_s, col_s, plane_ref, col_ref, psi_ref, pot_ref, beta_ref, coup_ref,
    zt_ref, yf_ref, xf_ref, xb_ref, yb_ref,
    out_ref,
    lenb, colb, psi2, z_tab, send1, recv1, send2, recv2,
    chi_f, chi_b, yhot, v3, dense, box, boxes, picked,
    gath, beta_f, beta_t, psi_f, psi_t, part_send, part_recv, term_f, term_send, term_recv,
    s1, r1, s2, r2, sg, rg, sp, rp, sn, rn,
):
    f = lax.axis_index("fft")
    g = lax.axis_index("band")
    nb = 2
    tot = n_fft * SLOTS
    nq = 2 * PLANES
    groups = n_fft // 8

    barrier = pltpu.get_barrier_semaphore()

    @pl.loop(1, n_fft)
    def _(k):
        pl.semaphore_signal(barrier, inc=1, device_id={"fft": lax.rem(f + k, n_fft)}, device_id_type=MESH)

    @pl.loop(1, n_band)
    def _(k):
        pl.semaphore_signal(barrier, inc=1, device_id={"band": lax.rem(g + k, n_band)}, device_id_type=MESH)

    @pl.loop(0, SLOTS)
    def _(s):
        lenb[pl.ds(s, 1), :] = jnp.full((1, W), len_s[f * SLOTS + s], jnp.int32)
        colb[pl.ds(s, 1), :] = jnp.full((1, W), col_s[f * SLOTS + s], jnp.int32)

    wave_z = iota((SLOTS, W), 1) - RAD
    in_sphere = (2 * jnp.abs(wave_z) < lenb[...]).astype(F32)
    psi2[...] = jnp.zeros(psi2.shape, BF16)
    for b in range(nb):
        for c in range(2):
            psi2[b, 0:SLOTS, c * W:(c + 1) * W] = (psi_ref[b, c].astype(F32) * in_sphere).astype(BF16)

    n_slot = n_fft * PLANES
    hot_z = (iota((256, n_slot), 0) == plane_ref[...]).astype(F32).T.astype(BF16)
    z_re = dot(hot_z, zt_ref[0]).reshape(n_fft, 1, PLANES, 256)
    z_im = dot(hot_z, zt_ref[1]).reshape(n_fft, 1, PLANES, 256)
    z_tab[...] = jnp.concatenate([z_re, z_im], axis=1).reshape(n_fft * nq, 256).astype(BF16)
    for b in range(nb):
        along = dot(z_tab[...], psi2[b], NT)
        send1[b] = along.reshape(n_fft, nq, W).astype(BF16)
        recv1[b, f] = send1[b, f]

    pl.semaphore_wait(barrier, n_fft + n_band - 2)

    def exchange(send, recv, send_sem, recv_sem, b):
        @pl.loop(1, n_fft)
        def _(k):
            e = lax.rem(f + k, n_fft)
            pltpu.make_async_remote_copy(
                src_ref=send.at[b, e], dst_ref=recv.at[b, f], send_sem=send_sem.at[b], recv_sem=recv_sem.at[b],
                device_id={"fft": e}, device_id_type=MESH,
            ).start()

    def wait_bytes(ref, sem):
        pltpu.make_async_copy(ref, ref, sem).wait()

    exchange(send1, recv1, s1, r1, 0)

    @pl.loop(1, n_band)
    def _(k):
        pltpu.make_async_remote_copy(
            src_ref=psi_ref, dst_ref=gath.at[g], send_sem=sg, recv_sem=rg,
            device_id={"band": lax.rem(g + k, n_band)}, device_id_type=MESH,
        ).start()

    exchange(send1, recv1, s1, r1, 1)
    gath[g] = psi_ref[...]

    def place_tables():
        for r in range(tot // W):
            col = col_ref[r:r + 1, :]
            c, d = col // W, col % W
            low = jnp.broadcast_to(c % LOW, (nq, W)).astype(F32)
            chi_f[:, r * W:(r + 1) * W] = low[:8]
            chi_b[:, r * W:(r + 1) * W] = low.astype(BF16)
            yhot[:, r * W:(r + 1) * W] = (iota((2 * W, W), 0) == (c // LOW) * W + d).astype(F32).astype(BF16)

    def potential_rows():
        @pl.loop(0, NG // 24)
        def _(m3):
            for u in range(3):
                m = m3 * 3 + u
                for r in range(8):
                    start = 240 * r
                    low = start // W * W
                    width = 256 if start - low <= 16 else 384
                    piece = pot_ref[:, pl.ds(pl.multiple_of(m * 1920 + low, W), width)]
                    if start - low:
                        piece = pltpu.roll(piece, width - (start - low), 1)
                    for c in range(2):
                        v3[c, pl.ds(pl.multiple_of((m * 8 + r) * 8, 8), 8), :] = piece[:, c * W:(c + 1) * W]

    def projector_rows():
        for k in range(8):
            for c in range(2):
                beta_f[pl.ds((c * 8 + k) * PAD, SLOTS), :] = beta_ref[0, k, c].astype(F32) * in_sphere

        @pl.loop(0, SLOTS // 4)
        def _(s4):
            for u in range(4):
                s = s4 * 4 + u
                rows = beta_f[pl.ds(s, 16, stride=PAD), :]
                beta_t[:, pl.ds(pl.multiple_of(s * W, W), W)] = rows.astype(BF16)

    lane16 = iota((nq, W), 1)

    def to_planes(b):
        wait_bytes(recv1.at[b, pl.ds(0, n_fft - 1)], r1.at[b])

    def spread_sticks(b):
        @pl.loop(0, groups)
        def _(h):
            outs = [jnp.zeros((nq, W), F32)] * 5
            for i in range(8):
                piece = recv1[b, h * 8 + i].astype(F32)
                off = 80 * i % W
                first = 80 * i // W
                rolled = pltpu.roll(piece, off, 1) if off else piece
                top = min(off + 80, W)
                outs[first] = jnp.where((lane16 >= off) & (lane16 < top), rolled, outs[first])
                if off + 80 > W:
                    outs[first + 1] = jnp.where(lane16 < off + 80 - W, rolled, outs[first + 1])
            at = pl.ds(pl.multiple_of(h * 640, W), 640)
            dense[:, at] = jnp.concatenate(outs, axis=1).astype(BF16)

    def place_columns(b):
        @pl.loop(0, 2)
        def _(m):
            first = (m * (LOW // 2)).astype(F32).astype(BF16)
            sticks = dense[...]
            place = chi_b[...] - first
            rows = [jnp.where(place == jnp.asarray(i, BF16), sticks, jnp.asarray(0, BF16)) for i in range(LOW // 2)]
            placed = dot(jnp.concatenate(rows, axis=0), yhot[...], NT)
            at = pl.ds(pl.multiple_of(m * (LOW // 2 * nq), LOW // 2 * nq), LOW // 2 * nq)
            for h in range(2):
                box[h, at, :] = placed[:, h * W:(h + 1) * W]

    def transform():
        @pl.loop(0, PLANES // 4)
        def _(quad):
            along_x = []
            for p in range(2):
                pair = []
                for u in range(2):
                    t = quad * 4 + p * 2 + u
                    pair.append(jnp.concatenate([box[h, pl.ds(t, W, stride=PLANES), :] for h in range(2)], axis=0))
                wide = dot(xf_ref[...], jnp.concatenate(pair, axis=1).astype(BF16)).astype(BF16)
                for u in range(2):
                    part = wide[:, u * W:(u + 1) * W]
                    along_x.append(jnp.concatenate([part[:NG], part[NG:]], axis=1))
            full = dot(jnp.concatenate(along_x, axis=0), yf_ref[...])
            weighted = []
            for u in range(4):
                weight = [v3[c, pl.ds(quad * 4 + u, NG, stride=PLANES), :] for c in range(2)]
                weighted.append((full[u * NG:(u + 1) * NG] * jnp.concatenate(weight * 2, axis=1)).astype(BF16))
            back = dot(jnp.concatenate(weighted, axis=0), yb_ref[...]).astype(BF16)
            for p in range(2):
                pair = [back[(p * 2 + u) * NG:(p * 2 + u + 1) * NG] for u in range(2)]
                pair = [jnp.concatenate([part[:, :W], part[:, W:]], axis=0) for part in pair]
                wide = dot(xb_ref[...], jnp.concatenate(pair, axis=1))
                for u in range(2):
                    t = quad * 4 + p * 2 + u
                    for h in range(2):
                        box[h, pl.ds(t, W, stride=PLANES), :] = wide[h * W:(h + 1) * W, u * W:(u + 1) * W]

    def to_sticks(b):
        boxes[...] = jnp.concatenate([box[0], box[1]], axis=1).astype(BF16)

        step = 512 if tot % 512 == 0 else 640

        @pl.loop(0, tot // step)
        def _(h):
            at = pl.ds(pl.multiple_of(h * step, W), step)
            rows = dot(boxes[...], yhot[:, at])
            place = jnp.concatenate([chi_f[:, at]] * 2, axis=0)
            found = jnp.zeros((nq, step), F32)
            for i in range(LOW):
                found = jnp.where(place == float(i), rows[i * nq:(i + 1) * nq], found)
            picked[:, at] = found

        @pl.loop(0, groups)
        def _(h):
            at = pl.ds(pl.multiple_of(h * 640, W), 640)
            found = picked[:, at]
            for i in range(8):
                off = 80 * i % W
                first = 80 * i // W
                piece = found[:, first * W:(first + 1) * W]
                if off:
                    piece = pltpu.roll(piece, W - off, 1)
                if off + 80 > W:
                    other = pltpu.roll(found[:, (first + 1) * W:(first + 2) * W], W - off, 1)
                    piece = jnp.where(lane16 < W - off, piece, other)
                send2[b, h * 8 + i] = jnp.where(lane16 < 80, piece, 0.0).astype(BF16)

        recv2[b, f] = send2[b, f]
        exchange(send2, recv2, s2, r2, b)

    nbr = 2 * nb * n_band
    swap = (
        ((iota((nbr, nbr), 0) == iota((nbr, nbr), 1) + 1) & (iota((nbr, nbr), 0) % 2 == 1)).astype(F32)
        - ((iota((nbr, nbr), 0) + 1 == iota((nbr, nbr), 1)) & (iota((nbr, nbr), 0) % 2 == 0)).astype(F32)
    )

    def project():
        wait_bytes(gath.at[pl.ds(0, n_band - 1)], rg)
        @pl.loop(0, n_band)
        def _(h):
            for b in range(nb):
                for c in range(2):
                    psi_f[pl.ds(pl.multiple_of((h * 4 + b * 2 + c) * PAD, 8), SLOTS), :] = gath[h, b, c].astype(F32)

        @pl.loop(0, SLOTS // 4)
        def _(s4):
            for u in range(4):
                s = s4 * 4 + u
                psi_t[:, pl.ds(pl.multiple_of(s * W, W), W)] = psi_f[pl.ds(s, nbr, stride=PAD), :].astype(BF16)

        prod = dot(beta_t[...], psi_t[...], NT)
        part = prod[:8] + dot(prod[8:], swap, precision=lax.Precision.HIGHEST)
        part_send[...] = jnp.zeros((8, W), F32)
        part_send[:, :nbr] = part
        part_recv[f] = part_send[...]

        @pl.loop(1, n_fft)
        def _(k):
            pltpu.make_async_remote_copy(
                src_ref=part_send, dst_ref=part_recv.at[f], send_sem=sp, recv_sem=rp,
                device_id={"fft": lax.rem(f + k, n_fft)}, device_id_type=MESH,
            ).start()

    def expand():
        wait_bytes(part_recv.at[pl.ds(0, n_fft - 1)], rp)
        whole = jnp.sum(part_recv[...], axis=0)[:, :nbr]
        coeffs = dot(coup_ref[g], whole, precision=lax.Precision.HIGHEST).astype(BF16).astype(F32)
        crossed = dot(coeffs, swap, precision=lax.Precision.HIGHEST)
        factors = jnp.concatenate([coeffs, -crossed], axis=0).astype(BF16)

        @pl.loop(0, SLOTS // 8)
        def _(m):
            terms = dot(factors, beta_t[:, pl.ds(pl.multiple_of(m * 1024, 1024), 1024)], TN)
            for i in range(8):
                term_f[pl.ds(m * 8 + i, nbr, stride=PAD), :] = terms[:, i * W:(i + 1) * W]

        @pl.loop(0, n_band)
        def _(h):
            for i in range(4):
                term_send[h, i * SLOTS:(i + 1) * SLOTS, :] = term_f[pl.ds(pl.multiple_of((h * 4 + i) * PAD, 8), SLOTS), :].astype(BF16)

        term_recv[g] = term_send[g]

        @pl.loop(1, n_band)
        def _(k):
            e = lax.rem(g + k, n_band)
            pltpu.make_async_remote_copy(
                src_ref=term_send.at[e], dst_ref=term_recv.at[g], send_sem=sn, recv_sem=rn,
                device_id={"band": e}, device_id_type=MESH,
            ).start()

    place_tables()
    potential_rows()
    projector_rows()
    to_planes(0)
    spread_sticks(0)
    place_columns(0)
    transform()
    project()
    to_sticks(0)
    to_planes(1)
    spread_sticks(1)
    place_columns(1)
    transform()
    expand()
    to_sticks(1)

    gx, gy = colb[...] // W - RAD, colb[...] % W - RAD
    kinetic = (gx * gx + gy * gy + wave_z * wave_z).astype(F32) / float(RAD * RAD)
    wait_bytes(term_recv.at[pl.ds(0, n_band - 1)], rn)
    for b in range(nb):
        wait_bytes(recv2.at[b, pl.ds(0, n_fft - 1)], r2.at[b])
        local = dot(recv2[b].reshape(n_fft * nq, W), z_tab[...], TN) * (1.0 / float(NG**3))
        for c in range(2):
            at = pl.ds((b * 2 + c) * SLOTS, SLOTS)
            nonlocal_sum = term_recv[0, at, :].astype(F32)
            for h in range(1, n_band):
                nonlocal_sum = nonlocal_sum + term_recv[h, at, :].astype(F32)
            wave = psi_ref[b, c].astype(F32) * in_sphere
            out_ref[b, c] = in_sphere * (kinetic * wave + local[:SLOTS, c * W:(c + 1) * W] + nonlocal_sum)

    for b in range(nb):
        wait_bytes(send1.at[b, pl.ds(0, n_fft - 1)], s1.at[b])
        wait_bytes(send2.at[b, pl.ds(0, n_fft - 1)], s2.at[b])
    wait_bytes(gath.at[pl.ds(0, n_band - 1)], sg)
    wait_bytes(part_recv.at[pl.ds(0, n_fft - 1)], sp)
    wait_bytes(term_send.at[pl.ds(0, n_band - 1)], sn)


def body(n_band, n_fft, psi, stick_col, stick_len, plane_z, potential, beta, coupling):
    tot = n_fft * SLOTS
    n_slot = n_fft * PLANES
    nq = 2 * PLANES
    nbr = 4 * n_band
    consts = [jnp.asarray(t) for t in tables()]
    vmem = pl.BlockSpec(memory_space=pltpu.VMEM)
    smem = pl.BlockSpec(memory_space=pltpu.SMEM)
    dma = pltpu.SemaphoreType.DMA
    return pl.pallas_call(
        functools.partial(kernel, n_band, n_fft),
        out_shape=jax.ShapeDtypeStruct(psi.shape, F32),
        in_specs=[smem, smem] + [vmem] * 11,
        out_specs=vmem,
        scratch_shapes=[
            pltpu.VMEM((SLOTS, W), jnp.int32),
            pltpu.VMEM((SLOTS, W), jnp.int32),
            pltpu.VMEM((2, W, 2 * W), BF16),
            pltpu.VMEM((n_fft * nq, 2 * W), BF16),
            pltpu.VMEM((2, n_fft, nq, W), BF16),
            pltpu.VMEM((2, n_fft, nq, W), BF16),
            pltpu.VMEM((2, n_fft, nq, W), BF16),
            pltpu.VMEM((2, n_fft, nq, W), BF16),
            pltpu.VMEM((8, tot), F32),
            pltpu.VMEM((nq, tot), BF16),
            pltpu.VMEM((2 * W, tot), BF16),
            pltpu.VMEM((2, NG * PLANES, W), F32),
            pltpu.VMEM((nq, tot), BF16),
            pltpu.VMEM((2, LOW * nq, W), F32),
            pltpu.VMEM((LOW * nq, 2 * W), BF16),
            pltpu.VMEM((nq, tot), F32),
            pltpu.VMEM((n_band, 2, 2, SLOTS, W), BF16),
            pltpu.VMEM((16 * PAD, W), F32),
            pltpu.VMEM((16, SLOTS * W), BF16),
            pltpu.VMEM((nbr * PAD, W), F32),
            pltpu.VMEM((nbr, SLOTS * W), BF16),
            pltpu.VMEM((8, W), F32),
            pltpu.VMEM((n_fft, 8, W), F32),
            pltpu.VMEM((nbr * PAD, W), F32),
            pltpu.VMEM((n_band, 4 * SLOTS, W), BF16),
            pltpu.VMEM((n_band, 4 * SLOTS, W), BF16),
            dma((2,)), dma((2,)), dma((2,)), dma((2,)),
            dma, dma, dma, dma, dma, dma,
        ],
        compiler_params=pltpu.CompilerParams(
            collective_id=0, has_side_effects=True, vmem_limit_bytes=56 * 1024 * 1024
        ),
    )(
        stick_len, stick_col, plane_z.reshape(1, n_slot), stick_col.reshape(tot // W, W),
        psi, potential, beta, coupling, *consts,
    )


def solution(mesh):
    in_specs = (
        P("band", None, "fft", None),
        P(),
        P(),
        P(),
        P("fft", None),
        P("band", None, None, "fft", None),
        P(),
    )
    out_specs = P("band", None, "fft", None)
    part = functools.partial(body, mesh.shape["band"], mesh.shape["fft"])
    return jax.shard_map(part, mesh=mesh, in_specs=in_specs, out_specs=out_specs, check_vma=False)
```

```python
import functools
import math

import jax
import jax.numpy as jnp
import numpy as np
from jax import lax
from jax.experimental import pallas as pl
from jax.experimental.pallas import tpu as pltpu
from jax.sharding import PartitionSpec as P

NG = 240
RAD = 60
W = 128
SLOTS = 80
PLANES = 8
LOW = 64
PAD = 88
F32 = jnp.float32
BF16 = jnp.bfloat16
MESH = pl.DeviceIdType.MESH


def tables():
    wave = np.arange(W) - RAD
    pos = np.arange(256)
    angle = 2.0 * np.pi * ((wave[:, None] * pos[None, :]) % NG) / NG
    inside = (pos < NG)[None, :]
    co, si = np.cos(angle) * inside, np.sin(angle) * inside
    z_re = np.concatenate([co.T, -si.T], axis=1)
    z_im = np.concatenate([si.T, co.T], axis=1)
    y_out = np.block([[co, si], [-si, co]])
    y_back = y_out.T
    cx, sx = co[:, :NG].T, si[:, :NG].T
    x_out = np.block([[cx, -sx], [sx, cx]])
    x_out = x_out.reshape(2 * NG, 2, W).transpose(0, 2, 1).reshape(2 * NG, 2 * W)
    x_back = x_out.T
    return [np.asarray(t, np.float32).astype(jnp.bfloat16) for t in (np.stack([z_re, z_im]), y_out, x_out, x_back, y_back)]


def iota(shape, dim):
    return lax.broadcasted_iota(jnp.int32, shape, dim)


def dot(a, b, dims=((1,), (0,)), precision=None):
    return lax.dot_general(a, b, (dims, ((), ())), preferred_element_type=F32, precision=precision)


NT = ((1,), (1,))
TN = ((0,), (0,))


def kernel(
    n_band, n_fft,
    len_h, col_h, plane_h, col2_h, psi_h, pot_h, beta_h, coup_h, zt_h, yf_h, xf_h, xb_h, yb_h,
    out_h,
    len_s, col_s, plane_ref, col_ref, psi_ref, pot_ref, beta_ref, coup_ref, zt_ref, yf_ref, xf_ref, xb_ref, yb_ref, out_ref,
    lenb, colb, psi2, z_tab, send1, recv1, send2, recv2,
    chi_f, chi_b, yhot, v3, dense, box, boxes, picked,
    gath, beta_f, beta_t, psi_f, psi_t, part_send, part_recv, term_f, term_send, term_recv, base,
    s1, r1, s2, r2, sg, rg, sp, rp, sn, rn, load_sem, out_sem,
):
    f = lax.axis_index("fft")
    g = lax.axis_index("band")
    nb = 2
    tot = n_fft * SLOTS
    nq = 2 * PLANES
    groups = n_fft // 8

    barrier = pltpu.get_barrier_semaphore()

    @pl.loop(1, n_fft)
    def _(k):
        pl.semaphore_signal(barrier, inc=1, device_id={"fft": lax.rem(f + k, n_fft)}, device_id_type=MESH)

    @pl.loop(1, n_band)
    def _(k):
        pl.semaphore_signal(barrier, inc=1, device_id={"band": lax.rem(g + k, n_band)}, device_id_type=MESH)

    pairs = (
        (len_h, len_s), (col_h, col_s), (plane_h, plane_ref), (psi_h, psi_ref), (zt_h, zt_ref), (col2_h, col_ref), (pot_h, pot_ref),
        (beta_h, beta_ref), (xf_h, xf_ref), (yf_h, yf_ref), (yb_h, yb_ref), (xb_h, xb_ref), (coup_h, coup_ref),
    )
    loads = [pltpu.make_async_copy(far, near, load_sem.at[i]) for i, (far, near) in enumerate(pairs)]
    for load in loads:
        load.start()
    for load in loads[:5]:
        load.wait()

    @pl.loop(0, SLOTS, unroll=8)
    def _(s):
        lenb[pl.ds(s, 1), :] = jnp.full((1, W), len_s[f * SLOTS + s], jnp.int32)
        colb[pl.ds(s, 1), :] = jnp.full((1, W), col_s[f * SLOTS + s], jnp.int32)

    wave_z = iota((SLOTS, W), 1) - RAD
    in_sphere = (2 * jnp.abs(wave_z) < lenb[...]).astype(F32)
    psi2[...] = jnp.zeros(psi2.shape, BF16)
    for b in range(nb):
        for c in range(2):
            psi2[b, 0:SLOTS, c * W:(c + 1) * W] = (psi_ref[b, c].astype(F32) * in_sphere).astype(BF16)

    n_slot = n_fft * PLANES
    hot_z = (iota((256, n_slot), 0) == plane_ref[...]).astype(F32).T.astype(BF16)
    z_re = dot(hot_z, zt_ref[0]).reshape(n_fft, 1, PLANES, 256)
    z_im = dot(hot_z, zt_ref[1]).reshape(n_fft, 1, PLANES, 256)
    z_tab[...] = jnp.concatenate([z_re, z_im], axis=1).reshape(n_fft * nq, 256).astype(BF16)
    for b in range(nb):
        along = dot(z_tab[...], psi2[b], NT)
        send1[b] = along.reshape(n_fft, nq, W).astype(BF16)
        recv1[b, f] = send1[b, f]

    pl.semaphore_wait(barrier, n_fft + n_band - 2)

    def exchange(send, recv, send_sem, recv_sem, b):
        @pl.loop(1, n_fft)
        def _(k):
            e = lax.rem(f + k, n_fft)
            pltpu.make_async_remote_copy(
                src_ref=send.at[b, e], dst_ref=recv.at[b, f], send_sem=send_sem.at[b], recv_sem=recv_sem.at[b],
                device_id={"fft": e}, device_id_type=MESH,
            ).start()

    def wait_bytes(ref, sem):
        pltpu.make_async_copy(ref, ref, sem).wait()

    exchange(send1, recv1, s1, r1, 0)

    @pl.loop(1, n_band)
    def _(k):
        pltpu.make_async_remote_copy(
            src_ref=psi_ref, dst_ref=gath.at[g], send_sem=sg, recv_sem=rg,
            device_id={"band": lax.rem(g + k, n_band)}, device_id_type=MESH,
        ).start()

    exchange(send1, recv1, s1, r1, 1)
    gath[g] = psi_ref[...]

    def place_tables():
        for r in range(tot // W):
            col = col_ref[r:r + 1, :]
            c, d = col // W, col % W
            low = jnp.broadcast_to(c % LOW, (nq, W)).astype(F32)
            chi_f[:, r * W:(r + 1) * W] = low[:8]
            chi_b[:, r * W:(r + 1) * W] = low.astype(BF16)
            yhot[:, r * W:(r + 1) * W] = (iota((2 * W, W), 0) == (c // LOW) * W + d).astype(F32).astype(BF16)

    def diagonal():
        gx, gy = colb[...] // W - RAD, colb[...] % W - RAD
        kinetic = (gx * gx + gy * gy + wave_z * wave_z).astype(F32) / float(RAD * RAD)
        for b in range(nb):
            for c in range(2):
                base[b, c] = kinetic * in_sphere * psi_ref[b, c].astype(F32)

    def potential_rows():
        @pl.loop(0, NG // 24)
        def _(m3):
            for u in range(3):
                m = m3 * 3 + u
                for r in range(8):
                    start = 240 * r
                    low = start // W * W
                    width = 256 if start - low <= 16 else 384
                    piece = pot_ref[:, pl.ds(pl.multiple_of(m * 1920 + low, W), width)]
                    if start - low:
                        piece = pltpu.roll(piece, width - (start - low), 1)
                    for c in range(2):
                        v3[c, pl.ds(pl.multiple_of((m * 8 + r) * 8, 8), 8), :] = piece[:, c * W:(c + 1) * W]

    def projector_rows():
        for k in range(8):
            for c in range(2):
                beta_f[pl.ds((c * 8 + k) * PAD, SLOTS), :] = beta_ref[0, k, c].astype(F32) * in_sphere

        @pl.loop(0, SLOTS // 4)
        def _(s4):
            for u in range(4):
                s = s4 * 4 + u
                rows = beta_f[pl.ds(s, 16, stride=PAD), :]
                beta_t[:, pl.ds(pl.multiple_of(s * W, W), W)] = rows.astype(BF16)

    lane16 = iota((nq, W), 1)

    def to_planes(b):
        wait_bytes(recv1.at[b, pl.ds(0, n_fft - 1)], r1.at[b])

    def spread_sticks(b):
        @pl.loop(0, groups)
        def _(h):
            outs = [jnp.zeros((nq, W), F32)] * 5
            for i in range(8):
                piece = recv1[b, h * 8 + i].astype(F32)
                off = 80 * i % W
                first = 80 * i // W
                rolled = pltpu.roll(piece, off, 1) if off else piece
                top = min(off + 80, W)
                outs[first] = jnp.where((lane16 >= off) & (lane16 < top), rolled, outs[first])
                if off + 80 > W:
                    outs[first + 1] = jnp.where(lane16 < off + 80 - W, rolled, outs[first + 1])
            at = pl.ds(pl.multiple_of(h * 640, W), 640)
            dense[:, at] = jnp.concatenate(outs, axis=1).astype(BF16)

    def place_columns(b):
        @pl.loop(0, 2)
        def _(m):
            first = (m * (LOW // 2)).astype(F32).astype(BF16)
            sticks = dense[...]
            place = chi_b[...] - first
            rows = [jnp.where(place == jnp.asarray(i, BF16), sticks, jnp.asarray(0, BF16)) for i in range(LOW // 2)]
            placed = dot(jnp.concatenate(rows, axis=0), yhot[...], NT)
            at = pl.ds(pl.multiple_of(m * (LOW // 2 * nq), LOW // 2 * nq), LOW // 2 * nq)
            for h in range(2):
                box[h, at, :] = placed[:, h * W:(h + 1) * W]

    def transform():
        @pl.loop(0, PLANES // 4)
        def _(quad):
            along_x = []
            for p in range(2):
                pair = []
                for u in range(2):
                    t = quad * 4 + p * 2 + u
                    pair.append(jnp.concatenate([box[h, pl.ds(t, W, stride=PLANES), :] for h in range(2)], axis=0))
                wide = dot(xf_ref[...], jnp.concatenate(pair, axis=1).astype(BF16)).astype(BF16)
                for u in range(2):
                    part = wide[:, u * W:(u + 1) * W]
                    along_x.append(jnp.concatenate([part[:NG], part[NG:]], axis=1))
            full = dot(jnp.concatenate(along_x, axis=0), yf_ref[...])
            weighted = []
            for u in range(4):
                weight = [v3[c, pl.ds(quad * 4 + u, NG, stride=PLANES), :] for c in range(2)]
                weighted.append((full[u * NG:(u + 1) * NG] * jnp.concatenate(weight * 2, axis=1)).astype(BF16))
            back = dot(jnp.concatenate(weighted, axis=0), yb_ref[...]).astype(BF16)
            for p in range(2):
                pair = [back[(p * 2 + u) * NG:(p * 2 + u + 1) * NG] for u in range(2)]
                pair = [jnp.concatenate([part[:, :W], part[:, W:]], axis=0) for part in pair]
                wide = dot(xb_ref[...], jnp.concatenate(pair, axis=1))
                for u in range(2):
                    t = quad * 4 + p * 2 + u
                    for h in range(2):
                        box[h, pl.ds(t, W, stride=PLANES), :] = wide[h * W:(h + 1) * W, u * W:(u + 1) * W]

    def to_sticks(b):
        boxes[...] = jnp.concatenate([box[0], box[1]], axis=1).astype(BF16)

        step = 1280 if tot % 1280 == 0 else 640
        chunks, each = tot // step, step // SLOTS

        @pl.loop(0, chunks)
        def _(turn):
            h = lax.rem(turn + f // each, chunks)
            at = pl.ds(pl.multiple_of(h * step, W), step)
            rows = dot(boxes[...], yhot[:, at])
            place = jnp.concatenate([chi_f[:, at]] * 2, axis=0)
            found = jnp.zeros((nq, step), F32)
            for i in range(LOW):
                found = jnp.where(place == float(i), rows[i * nq:(i + 1) * nq], found)
            for i in range(each):
                off = 80 * i % W
                first = 80 * i // W
                piece = found[:, first * W:(first + 1) * W]
                if off:
                    piece = pltpu.roll(piece, W - off, 1)
                if off + 80 > W:
                    other = pltpu.roll(found[:, (first + 1) * W:(first + 2) * W], W - off, 1)
                    piece = jnp.where(lane16 < W - off, piece, other)
                send2[b, h * each + i] = jnp.where(lane16 < 80, piece, 0.0).astype(BF16)

            @pl.loop(0, each)
            def _(i):
                e = h * each + lax.rem(i + f, each)

                @pl.when(e != f)
                def _():
                    pltpu.make_async_remote_copy(
                        src_ref=send2.at[b, e], dst_ref=recv2.at[b, f], send_sem=s2.at[b], recv_sem=r2.at[b],
                        device_id={"fft": e}, device_id_type=MESH,
                    ).start()

        recv2[b, f] = send2[b, f]

    nbr = 2 * nb * n_band
    swap = (
        ((iota((nbr, nbr), 0) == iota((nbr, nbr), 1) + 1) & (iota((nbr, nbr), 0) % 2 == 1)).astype(F32)
        - ((iota((nbr, nbr), 0) + 1 == iota((nbr, nbr), 1)) & (iota((nbr, nbr), 0) % 2 == 0)).astype(F32)
    )

    def project():
        wait_bytes(gath.at[pl.ds(0, n_band - 1)], rg)
        @pl.loop(0, n_band)
        def _(h):
            for b in range(nb):
                for c in range(2):
                    psi_f[pl.ds(pl.multiple_of((h * 4 + b * 2 + c) * PAD, 8), SLOTS), :] = gath[h, b, c].astype(F32)

        @pl.loop(0, SLOTS // 4)
        def _(s4):
            for u in range(4):
                s = s4 * 4 + u
                psi_t[:, pl.ds(pl.multiple_of(s * W, W), W)] = psi_f[pl.ds(s, nbr, stride=PAD), :].astype(BF16)

        prod = dot(beta_t[...], psi_t[...], NT)
        part = prod[:8] + dot(prod[8:], swap, precision=lax.Precision.HIGHEST)
        part_send[...] = jnp.zeros((8, W), F32)
        part_send[:, :nbr] = part
        part_recv[f] = part_send[...]

        @pl.loop(1, n_fft)
        def _(k):
            pltpu.make_async_remote_copy(
                src_ref=part_send, dst_ref=part_recv.at[f], send_sem=sp, recv_sem=rp,
                device_id={"fft": lax.rem(f + k, n_fft)}, device_id_type=MESH,
            ).start()

    def expand():
        wait_bytes(part_recv.at[pl.ds(0, n_fft - 1)], rp)
        whole = jnp.sum(part_recv[...], axis=0)[:, :nbr]
        coeffs = dot(coup_ref[g], whole, precision=lax.Precision.HIGHEST).astype(BF16).astype(F32)
        crossed = dot(coeffs, swap, precision=lax.Precision.HIGHEST)
        factors = jnp.concatenate([coeffs, -crossed], axis=0).T.astype(BF16)

        @pl.loop(0, SLOTS // 16)
        def _(m):
            terms = dot(factors, beta_t[:, pl.ds(pl.multiple_of(m * 2048, 2048), 2048)])
            for i in range(16):
                term_f[pl.ds(m * 16 + i, nbr, stride=PAD), :] = terms[:, i * W:(i + 1) * W]

        @pl.loop(0, n_band)
        def _(h):
            for i in range(4):
                term_send[h, i * SLOTS:(i + 1) * SLOTS, :] = term_f[pl.ds(pl.multiple_of((h * 4 + i) * PAD, 8), SLOTS), :].astype(BF16)

        term_recv[g] = term_send[g]

        @pl.loop(1, n_band)
        def _(k):
            e = lax.rem(g + k, n_band)
            pltpu.make_async_remote_copy(
                src_ref=term_send.at[e], dst_ref=term_recv.at[g], send_sem=sn, recv_sem=rn,
                device_id={"band": e}, device_id_type=MESH,
            ).start()

    for load in loads[5:]:
        load.wait()
    diagonal()
    place_tables()
    potential_rows()
    projector_rows()
    to_planes(0)
    spread_sticks(0)
    place_columns(0)
    transform()
    project()
    to_sticks(0)
    to_planes(1)
    spread_sticks(1)
    place_columns(1)
    transform()
    expand()
    to_sticks(1)

    wait_bytes(term_recv.at[pl.ds(0, n_band - 1)], rn)
    for b in range(nb):
        for c in range(2):
            at = pl.ds((b * 2 + c) * SLOTS, SLOTS)
            nonlocal_sum = term_recv[0, at, :].astype(F32)
            for h in range(1, n_band):
                nonlocal_sum = nonlocal_sum + term_recv[h, at, :].astype(F32)
            base[b, c] = base[b, c] + in_sphere * nonlocal_sum

    stores = [pltpu.make_async_copy(out_ref.at[b], out_h.at[b], out_sem.at[b]) for b in range(nb)]
    for b in range(nb):
        wait_bytes(recv2.at[b, pl.ds(0, n_fft - 1)], r2.at[b])
        local = dot(recv2[b].reshape(n_fft * nq, W), z_tab[...], TN) * (1.0 / float(NG**3))
        for c in range(2):
            out_ref[b, c] = base[b, c] + in_sphere * local[:SLOTS, c * W:(c + 1) * W]
        stores[b].start()

    for b in range(nb):
        wait_bytes(send1.at[b, pl.ds(0, n_fft - 1)], s1.at[b])
        wait_bytes(send2.at[b, pl.ds(0, n_fft - 1)], s2.at[b])
    wait_bytes(gath.at[pl.ds(0, n_band - 1)], sg)
    wait_bytes(part_recv.at[pl.ds(0, n_fft - 1)], sp)
    wait_bytes(term_send.at[pl.ds(0, n_band - 1)], sn)
    for b in range(nb):
        stores[b].wait()


def body(n_band, n_fft, psi, stick_col, stick_len, plane_z, potential, beta, coupling):
    tot = n_fft * SLOTS
    n_slot = n_fft * PLANES
    nq = 2 * PLANES
    nbr = 4 * n_band
    consts = [jnp.asarray(t) for t in tables()]
    hbm = pl.BlockSpec(memory_space=pl.ANY)
    dma = pltpu.SemaphoreType.DMA
    operands = [
        stick_len, stick_col, plane_z.reshape(1, n_slot), stick_col.reshape(tot // W, W),
        psi, potential, beta, coupling, *consts,
    ]
    return pl.pallas_call(
        functools.partial(kernel, n_band, n_fft),
        out_shape=jax.ShapeDtypeStruct(psi.shape, F32),
        in_specs=[hbm] * len(operands),
        out_specs=hbm,
        scratch_shapes=[
            *[(pltpu.SMEM if i < 2 else pltpu.VMEM)(x.shape, x.dtype) for i, x in enumerate(operands)],
            pltpu.VMEM(psi.shape, F32),
            pltpu.VMEM((SLOTS, W), jnp.int32),
            pltpu.VMEM((SLOTS, W), jnp.int32),
            pltpu.VMEM((2, W, 2 * W), BF16),
            pltpu.VMEM((n_fft * nq, 2 * W), BF16),
            pltpu.VMEM((2, n_fft, nq, W), BF16),
            pltpu.VMEM((2, n_fft, nq, W), BF16),
            pltpu.VMEM((2, n_fft, nq, W), BF16),
            pltpu.VMEM((2, n_fft, nq, W), BF16),
            pltpu.VMEM((8, tot), F32),
            pltpu.VMEM((nq, tot), BF16),
            pltpu.VMEM((2 * W, tot), BF16),
            pltpu.VMEM((2, NG * PLANES, W), F32),
            pltpu.VMEM((nq, tot), BF16),
            pltpu.VMEM((2, LOW * nq, W), F32),
            pltpu.VMEM((LOW * nq, 2 * W), BF16),
            pltpu.VMEM((nq, tot), F32),
            pltpu.VMEM((n_band, 2, 2, SLOTS, W), BF16),
            pltpu.VMEM((16 * PAD, W), F32),
            pltpu.VMEM((16, SLOTS * W), BF16),
            pltpu.VMEM((nbr * PAD, W), F32),
            pltpu.VMEM((nbr, SLOTS * W), BF16),
            pltpu.VMEM((8, W), F32),
            pltpu.VMEM((n_fft, 8, W), F32),
            pltpu.VMEM((nbr * PAD, W), F32),
            pltpu.VMEM((n_band, 4 * SLOTS, W), BF16),
            pltpu.VMEM((n_band, 4 * SLOTS, W), BF16),
            pltpu.VMEM(psi.shape, F32),
            dma((2,)), dma((2,)), dma((2,)), dma((2,)),
            dma, dma, dma, dma, dma, dma, dma((len(operands),)), dma((2,)),
        ],
        compiler_params=pltpu.CompilerParams(
            collective_id=0, has_side_effects=True, vmem_limit_bytes=56 * 1024 * 1024
        ),
    )(*operands)


def solution(mesh):
    in_specs = (
        P("band", None, "fft", None),
        P(),
        P(),
        P(),
        P("fft", None),
        P("band", None, None, "fft", None),
        P(),
    )
    out_specs = P("band", None, "fft", None)
    part = functools.partial(body, mesh.shape["band"], mesh.shape["fft"])
    return jax.shard_map(part, mesh=mesh, in_specs=in_specs, out_specs=out_specs, check_vma=False)
```

```python
import functools
import math

import jax
import jax.numpy as jnp
import numpy as np
from jax import lax
from jax.experimental import pallas as pl
from jax.experimental.pallas import tpu as pltpu
from jax.sharding import PartitionSpec as P

NG = 240
RAD = 60
W = 128
SLOTS = 80
PLANES = 8
LOW = 64
PAD = 88
F32 = jnp.float32
BF16 = jnp.bfloat16
MESH = pl.DeviceIdType.MESH


def tables():
    wave = np.arange(W) - RAD
    pos = np.arange(256)
    angle = 2.0 * np.pi * ((wave[:, None] * pos[None, :]) % NG) / NG
    inside = (pos < NG)[None, :]
    co, si = np.cos(angle) * inside, np.sin(angle) * inside
    z_re = np.concatenate([co.T, -si.T], axis=1)
    z_im = np.concatenate([si.T, co.T], axis=1)
    y_out = np.block([[co, si], [-si, co]])
    y_back = y_out.T
    cx, sx = co[:, :NG].T, si[:, :NG].T
    x_out = np.block([[cx, -sx], [sx, cx]])
    x_out = x_out.reshape(2, NG // 16, 16, 2, W).transpose(1, 0, 2, 4, 3).reshape(2 * NG, 2 * W)
    x_back = x_out.T
    return [np.asarray(t, np.float32).astype(jnp.bfloat16) for t in (np.stack([z_re, z_im]), y_out, x_out, x_back, y_back)]


def iota(shape, dim):
    return lax.broadcasted_iota(jnp.int32, shape, dim)


def dot(a, b, dims=((1,), (0,)), precision=None):
    return lax.dot_general(a, b, (dims, ((), ())), preferred_element_type=F32, precision=precision)


NT = ((1,), (1,))
TN = ((0,), (0,))


def kernel(
    n_band, n_fft,
    len_h, col_h, plane_h, col2_h, len2_h, psi_h, pot_h, beta_h, coup_h, zt_h, yf_h, xf_h, xb_h, yb_h,
    out_h,
    len_s, col_s, plane_ref, col_ref, len_ref, psi_ref, pot_ref, beta_ref, coup_ref, zt_ref, yf_ref, xf_ref, xb_ref, yb_ref, out_ref,
    lenb, colb, psi2, z_tab, send1, recv1, send2, recv2,
    chi_f, chi_b, yhot, v3, dense, box, boxes, leave, come,
    gath, beta_other, beta_f, beta_t, psi_f, psi_t, product, part_send, part_recv, term_f, term_send, term_recv, base,
    s1, r1, s2, r2, sg, rg, sp, rp, sn, rn, sb, rb, load_sem, out_sem,
):
    f = lax.axis_index("fft")
    g = lax.axis_index("band")
    nb = 2
    tot = n_fft * SLOTS
    nq = 2 * PLANES
    cap = -(-tot // 2 // W) * W

    barrier = pltpu.get_barrier_semaphore()

    @pl.loop(1, n_fft)
    def _(k):
        pl.semaphore_signal(barrier, inc=1, device_id={"fft": lax.rem(f + k, n_fft)}, device_id_type=MESH)

    n_chip = n_band // 2
    chip = lax.div(g, 2)
    other = g + 1 - 2 * lax.rem(g, 2)

    def same_core(k):
        return lax.rem(g + 2 * k, n_band)

    pl.semaphore_signal(barrier, inc=1, device_id={"band": other}, device_id_type=MESH)
    for k in range(1, n_chip):
        pl.semaphore_signal(barrier, inc=1, device_id={"band": same_core(k)}, device_id_type=MESH)

    pairs = (
        (len_h, len_s), (col_h, col_s), (plane_h, plane_ref), (psi_h, psi_ref), (zt_h, zt_ref), (col2_h, col_ref), (len2_h, len_ref), (pot_h, pot_ref),
        (beta_h, beta_ref), (xf_h, xf_ref), (yf_h, yf_ref), (yb_h, yb_ref), (xb_h, xb_ref), (coup_h, coup_ref),
    )
    loads = [pltpu.make_async_copy(far, near, load_sem.at[i]) for i, (far, near) in enumerate(pairs)]
    for load in loads:
        load.start()
    for load in loads[:5]:
        load.wait()

    @pl.loop(0, SLOTS, unroll=8)
    def _(s):
        lenb[pl.ds(s, 1), :] = jnp.full((1, W), len_s[f * SLOTS + s], jnp.int32)
        colb[pl.ds(s, 1), :] = jnp.full((1, W), col_s[f * SLOTS + s], jnp.int32)

    wave_z = iota((SLOTS, W), 1) - RAD
    in_sphere = (2 * jnp.abs(wave_z) < lenb[...]).astype(F32)
    psi2[...] = jnp.zeros(psi2.shape, BF16)
    for b in range(nb):
        for c in range(2):
            psi2[b, 0:SLOTS, c * W:(c + 1) * W] = (psi_ref[b, c].astype(F32) * in_sphere).astype(BF16)

    n_slot = n_fft * PLANES
    hot_z = (iota((256, n_slot), 0) == plane_ref[...]).astype(F32).T.astype(BF16)
    z_re = dot(hot_z, zt_ref[0]).reshape(n_fft, 1, PLANES, 256)
    z_im = dot(hot_z, zt_ref[1]).reshape(n_fft, 1, PLANES, 256)
    z_tab[...] = jnp.concatenate([z_re, z_im], axis=1).reshape(n_fft * nq, 256).astype(BF16)
    for b in range(nb):
        along = dot(z_tab[...], psi2[b], NT)
        send1[b] = along.reshape(n_fft, nq, W).astype(BF16)
        recv1[b, f] = send1[b, f]

    pl.semaphore_wait(barrier, n_fft - 1 + n_chip)

    def exchange(send, recv, send_sem, recv_sem, b):
        @pl.loop(1, n_fft)
        def _(k):
            e = lax.rem(f + k, n_fft)
            pltpu.make_async_remote_copy(
                src_ref=send.at[b, e], dst_ref=recv.at[b, f], send_sem=send_sem.at[b], recv_sem=recv_sem.at[b],
                device_id={"fft": e}, device_id_type=MESH,
            ).start()

    def wait_bytes(ref, sem):
        pltpu.make_async_copy(ref, ref, sem).wait()

    exchange(send1, recv1, s1, r1, 0)

    def to_chips(k, src, dst, send_sem, recv_sem):
        return pltpu.make_async_remote_copy(
            src_ref=src, dst_ref=dst, send_sem=send_sem, recv_sem=recv_sem,
            device_id={"band": same_core(k)}, device_id_type=MESH,
        )

    for k in range(1, n_chip):
        to_chips(k, psi_ref, gath.at[chip], sg, rg).start()
    loads[8].wait()
    swap_beta = pltpu.make_async_remote_copy(
        src_ref=beta_ref, dst_ref=beta_other, send_sem=sb, recv_sem=rb, device_id={"band": other}, device_id_type=MESH
    )
    swap_beta.start()
    gath[chip] = psi_ref[...]

    bits = (n_fft * W - 1).bit_length()
    lane8 = iota((8, W), 1)

    def moved_left(cols, k):
        if k >= 7:
            far = 1 << (k - 7)
            return cols[far:] + [jnp.zeros_like(cols[0])] * min(far, len(cols))
        step = 1 << k
        rolled = [pltpu.roll(col, W - step, 1) for col in cols]
        lane = iota(cols[0].shape, 1)
        return [jnp.where(lane < W - step, one, two) for one, two in zip(rolled, rolled[1:] + [jnp.zeros_like(cols[0])])]

    def moved_right(cols, k):
        if k >= 7:
            far = 1 << (k - 7)
            return [jnp.zeros_like(cols[0])] * min(far, len(cols)) + cols[:max(len(cols) - far, 0)]
        step = 1 << k
        rolled = [pltpu.roll(col, step, 1) for col in cols]
        lane = iota(cols[0].shape, 1)
        return [jnp.where(lane >= step, one, two) for one, two in zip(rolled, [jnp.zeros_like(cols[0])] + rolled[:-1])]

    def place_tables():
        dense = []
        for r in range(tot // W):
            used = jnp.broadcast_to(len_ref[r:r + 1, :], (8, W)) > 0
            dense.append(jnp.where(used, jnp.broadcast_to(col_ref[r:r + 1, :], (8, W)), -1))
        cols, moves = [], []
        ahead = jnp.zeros((8, 1), F32)
        for e in range(n_fft):
            first, off = 80 * e // W, 80 * e % W
            piece = pltpu.roll(dense[first], W - off, 1) if off else dense[first]
            if off + 80 > W:
                piece = jnp.where(lane8 < W - off, piece, pltpu.roll(dense[first + 1], W - off, 1))
            piece = jnp.where(lane8 < 80, piece, -1)
            used = piece >= 0
            cols.append(piece)
            moves.append(jnp.where(used, jnp.broadcast_to(ahead, (8, W)), 0.0).astype(jnp.int32))
            ahead = ahead + (float(W) - jnp.sum(used.astype(F32), axis=1, keepdims=True))
        for k in range(bits):
            next_moves, next_cols = moved_left(moves, k), moved_left(cols, k)
            for e in range(n_fft):
                leaves, comes = (moves[e] >> k) & 1, (next_moves[e] >> k) & 1
                at = slice(e * W, (e + 1) * W)
                leave[k, :, at] = leaves
                come[k, :, at] = comes
                moves[e] = jnp.where(comes > 0, next_moves[e], jnp.where(leaves > 0, 0, moves[e]))
                cols[e] = jnp.where(comes > 0, next_cols[e], jnp.where(leaves > 0, -1, cols[e]))
        for r in range(cap // W):
            at = slice(r * W, (r + 1) * W)
            c, d = cols[r] >> 7, cols[r] & (W - 1)
            chi = (c & (LOW - 1)).astype(F32)
            chi_f[:, at] = chi
            chi_b[:, at] = jnp.concatenate([chi, chi], axis=0).astype(BF16)
            row = jnp.where(cols[r] < 0, -1, (c >> 6) * W + d)
            yhot[:, at] = (iota((2 * W, W), 0) == row[:1]).astype(F32).astype(BF16)

    def diagonal():
        gx, gy = colb[...] // W - RAD, colb[...] % W - RAD
        kinetic = (gx * gx + gy * gy + wave_z * wave_z).astype(F32) / float(RAD * RAD)
        for b in range(nb):
            for c in range(2):
                base[b, c] = kinetic * in_sphere * psi_ref[b, c].astype(F32)

    def potential_rows():
        @pl.loop(0, NG // 24)
        def _(m3):
            for u in range(3):
                m = m3 * 3 + u
                for r in range(8):
                    start = 240 * r
                    low = start // W * W
                    width = 256 if start - low <= 16 else 384
                    piece = pot_ref[:, pl.ds(pl.multiple_of(m * 1920 + low, W), width)]
                    if start - low:
                        piece = pltpu.roll(piece, width - (start - low), 1)
                    for c in range(2):
                        v3[c, pl.ds(pl.multiple_of((m * 8 + r) * 8, 8), 8), :] = piece[:, c * W:(c + 1) * W]

    def projector_rows():
        swap_beta.wait_recv()
        for a, source in enumerate((beta_ref, beta_other)):
            for k in range(8):
                for c in range(2):
                    beta_f[pl.ds((c * 16 + a * 8 + k) * PAD, SLOTS), :] = source[0, k, c].astype(F32) * in_sphere

        @pl.loop(0, SLOTS // 4)
        def _(s4):
            for u in range(4):
                s = s4 * 4 + u
                rows = beta_f[pl.ds(s, 32, stride=PAD), :]
                beta_t[:, pl.ds(pl.multiple_of(s * W, W), W)] = rows.astype(BF16)

    def to_planes(b):
        wait_bytes(recv1.at[b, pl.ds(0, n_fft - 1)], r1.at[b])

    def both(mask):
        return jnp.concatenate([mask, mask], axis=0)

    def pack_sticks(b):
        cols = [recv1[b, e].astype(F32) for e in range(n_fft)]
        for k in range(bits):
            arriving = moved_left(cols, k)
            cols = [jnp.where(both(come[k, :, e * W:(e + 1) * W]) > 0, arriving[e], cols[e]) for e in range(n_fft)]
        dense[...] = jnp.concatenate(cols[:cap // W], axis=1).astype(BF16)

    def place_columns(b):
        sticks, place = dense[...], chi_b[...]
        rows = [jnp.where(place == jnp.asarray(i, BF16), sticks, jnp.asarray(0, BF16)) for i in range(LOW)]
        placed = dot(jnp.concatenate(rows, axis=0), yhot[...], NT)
        for h in range(2):
            box[h] = placed[:, h * W:(h + 1) * W]

    def transform():
        @pl.loop(0, PLANES // 4)
        def _(quad):
            along_x = []
            for p in range(2):
                pair = []
                for u in range(2):
                    t = quad * 4 + p * 2 + u
                    pair.append(jnp.concatenate([box[h, pl.ds(t, W, stride=PLANES), :] for h in range(2)], axis=0))
                wide = dot(xf_ref[...], jnp.concatenate(pair, axis=1).astype(BF16)).astype(BF16)
                wide = wide.reshape(NG // 16, 2, 16, 2 * W)
                for u in range(2):
                    part = [wide[:, c, :, u * W:(u + 1) * W].reshape(NG, W) for c in range(2)]
                    along_x.append(jnp.concatenate(part, axis=1))
            full = dot(jnp.concatenate(along_x, axis=0), yf_ref[...])
            weighted = []
            for u in range(4):
                weight = [v3[c, pl.ds(quad * 4 + u, NG, stride=PLANES), :] for c in range(2)]
                weighted.append((full[u * NG:(u + 1) * NG] * jnp.concatenate(weight * 2, axis=1)).astype(BF16))
            back = dot(jnp.concatenate(weighted, axis=0), yb_ref[...]).astype(BF16)
            for p in range(2):
                pair = [back[(p * 2 + u) * NG:(p * 2 + u + 1) * NG] for u in range(2)]
                pair = [part.reshape(NG // 16, 1, 16, 2 * W) for part in pair]
                pair = [jnp.concatenate([part[..., :W], part[..., W:]], axis=1).reshape(2 * NG, W) for part in pair]
                wide = dot(xb_ref[...], jnp.concatenate(pair, axis=1))
                for u in range(2):
                    t = quad * 4 + p * 2 + u
                    for h in range(2):
                        box[h, pl.ds(t, W, stride=PLANES), :] = wide[h * W:(h + 1) * W, u * W:(u + 1) * W]

    def to_sticks(b):
        boxes[...] = jnp.concatenate([box[0], box[1]], axis=1).astype(BF16)

        rows = dot(boxes[...], yhot[...])
        place = both(chi_f[...])
        found = jnp.zeros((nq, cap), F32)
        for i in range(LOW):
            found = jnp.where(place == float(i), rows[i * nq:(i + 1) * nq], found)
        cols = [found[:, r * W:(r + 1) * W] for r in range(cap // W)]
        cols = cols + [jnp.zeros((nq, W), F32)] * (n_fft - len(cols))
        for k in reversed(range(bits)):
            leaving = moved_right(cols, k)
            cols = [jnp.where(both(leave[k, :, e * W:(e + 1) * W]) > 0, leaving[e], cols[e]) for e in range(n_fft)]
        for e in range(n_fft):
            send2[b, e] = cols[e].astype(BF16)
        recv2[b, f] = send2[b, f]
        exchange(send2, recv2, s2, r2, b)

    nbr = 2 * nb * n_chip

    def cross(x):
        return jnp.where(iota(x.shape, 1) % 2 == 0, pltpu.roll(x, W - 1, 1), -pltpu.roll(x, 1, 1))

    def project():
        if n_chip > 1:
            wait_bytes(gath.at[pl.ds(0, n_chip - 1)], rg)

        @pl.loop(0, n_chip)
        def _(h):
            for b in range(nb):
                for c in range(2):
                    psi_f[pl.ds(pl.multiple_of((h * 4 + b * 2 + c) * PAD, 8), SLOTS), :] = gath[h, b, c].astype(F32)

        @pl.loop(0, SLOTS // 8)
        def _(s8):
            for u in range(8):
                s = s8 * 8 + u
                psi_t[:, pl.ds(pl.multiple_of(s * W, W), W)] = psi_f[pl.ds(s, nbr, stride=PAD), :].astype(BF16)

        product[...] = jnp.zeros(product.shape, F32)
        product[:, :nbr] = dot(beta_t[...], psi_t[...], NT)
        one, two = [product[a * 8:a * 8 + 8] + cross(product[16 + a * 8:24 + a * 8]) for a in range(2)]
        part_send[...] = jnp.where(lane8 < nbr, one, pltpu.roll(two, nbr, 1))
        part_recv[f] = part_send[...]

        @pl.loop(1, n_fft)
        def _(k):
            pltpu.make_async_remote_copy(
                src_ref=part_send, dst_ref=part_recv.at[f], send_sem=sp, recv_sem=rp,
                device_id={"fft": lax.rem(f + k, n_fft)}, device_id_type=MESH,
            ).start()

    def expand():
        wait_bytes(part_recv.at[pl.ds(0, n_fft - 1)], rp)
        whole = jnp.sum(part_recv[...], axis=0)
        coupling = jnp.concatenate([coup_ref[g], coup_ref[other]], axis=0)
        coupled = dot(coupling, whole, precision=lax.Precision.HIGHEST)
        coeffs = jnp.where(lane8 < nbr, coupled[:8], coupled[8:]).astype(BF16).astype(F32)
        crossed = -cross(coeffs)
        factors = [x if a == 0 else pltpu.roll(x, W - nbr, 1) for x in (coeffs, crossed) for a in range(2)]
        factors = jnp.concatenate(factors + [jnp.zeros((W - 32, W), F32)], axis=0).T[:nbr, :32].astype(BF16)

        @pl.loop(0, SLOTS // 16)
        def _(m):
            terms = dot(factors, beta_t[:, pl.ds(pl.multiple_of(m * 2048, 2048), 2048)])
            for i in range(16):
                term_f[pl.ds(m * 16 + i, nbr, stride=PAD), :] = terms[:, i * W:(i + 1) * W]

        for k in reversed(range(n_chip)):
            h = lax.div(same_core(k), 2)
            for i in range(4):
                at = pl.ds(pl.multiple_of((h * 4 + i) * PAD, 8), SLOTS)
                term_send[h, i * SLOTS:(i + 1) * SLOTS, :] = term_f[at, :].astype(BF16)
            if k:
                to_chips(k, term_send.at[h], term_recv.at[chip], sn, rn).start()
            else:
                term_recv[chip] = term_send[chip]

    for load in loads[5:8] + loads[9:]:
        load.wait()
    diagonal()
    place_tables()
    potential_rows()
    projector_rows()
    to_planes(0)
    exchange(send1, recv1, s1, r1, 1)
    pack_sticks(0)
    place_columns(0)
    project()
    transform()
    to_sticks(0)
    to_planes(1)
    pack_sticks(1)
    place_columns(1)
    transform()
    expand()
    to_sticks(1)

    if n_chip > 1:
        wait_bytes(term_recv.at[pl.ds(0, n_chip - 1)], rn)
    for b in range(nb):
        for c in range(2):
            at = pl.ds((b * 2 + c) * SLOTS, SLOTS)
            nonlocal_sum = term_recv[0, at, :].astype(F32)
            for h in range(1, n_chip):
                nonlocal_sum = nonlocal_sum + term_recv[h, at, :].astype(F32)
            base[b, c] = base[b, c] + in_sphere * nonlocal_sum

    stores = [pltpu.make_async_copy(out_ref.at[b], out_h.at[b], out_sem.at[b]) for b in range(nb)]
    for b in range(nb):
        wait_bytes(recv2.at[b, pl.ds(0, n_fft - 1)], r2.at[b])
        local = dot(recv2[b].reshape(n_fft * nq, W), z_tab[...], TN) * (1.0 / float(NG**3))
        for c in range(2):
            out_ref[b, c] = base[b, c] + in_sphere * local[:SLOTS, c * W:(c + 1) * W]
        stores[b].start()

    for b in range(nb):
        wait_bytes(send1.at[b, pl.ds(0, n_fft - 1)], s1.at[b])
        wait_bytes(send2.at[b, pl.ds(0, n_fft - 1)], s2.at[b])
    if n_chip > 1:
        wait_bytes(gath.at[pl.ds(0, n_chip - 1)], sg)
        wait_bytes(term_send.at[pl.ds(0, n_chip - 1)], sn)
    wait_bytes(part_recv.at[pl.ds(0, n_fft - 1)], sp)
    swap_beta.wait_send()
    for b in range(nb):
        stores[b].wait()


def body(n_band, n_fft, psi, stick_col, stick_len, plane_z, potential, beta, coupling):
    tot = n_fft * SLOTS
    n_slot = n_fft * PLANES
    nq = 2 * PLANES
    n_chip = n_band // 2
    nbr = 4 * n_chip
    cap = -(-tot // 2 // W) * W
    consts = [jnp.asarray(t) for t in tables()]
    hbm = pl.BlockSpec(memory_space=pl.ANY)
    dma = pltpu.SemaphoreType.DMA
    operands = [
        stick_len, stick_col, plane_z.reshape(1, n_slot), stick_col.reshape(tot // W, W), stick_len.reshape(tot // W, W),
        psi, potential, beta, coupling, *consts,
    ]
    return pl.pallas_call(
        functools.partial(kernel, n_band, n_fft),
        out_shape=jax.ShapeDtypeStruct(psi.shape, F32),
        in_specs=[hbm] * len(operands),
        out_specs=hbm,
        scratch_shapes=[
            *[(pltpu.SMEM if i < 2 else pltpu.VMEM)(x.shape, x.dtype) for i, x in enumerate(operands)],
            pltpu.VMEM(psi.shape, F32),
            pltpu.VMEM((SLOTS, W), jnp.int32),
            pltpu.VMEM((SLOTS, W), jnp.int32),
            pltpu.VMEM((2, W, 2 * W), BF16),
            pltpu.VMEM((n_fft * nq, 2 * W), BF16),
            pltpu.VMEM((2, n_fft, nq, W), BF16),
            pltpu.VMEM((2, n_fft, nq, W), BF16),
            pltpu.VMEM((2, n_fft, nq, W), BF16),
            pltpu.VMEM((2, n_fft, nq, W), BF16),
            pltpu.VMEM((8, cap), F32),
            pltpu.VMEM((nq, cap), BF16),
            pltpu.VMEM((2 * W, cap), BF16),
            pltpu.VMEM((2, NG * PLANES, W), F32),
            pltpu.VMEM((nq, cap), BF16),
            pltpu.VMEM((2, LOW * nq, W), F32),
            pltpu.VMEM((LOW * nq, 2 * W), BF16),
            pltpu.VMEM(((n_fft * W - 1).bit_length(), 8, n_fft * W), jnp.int32),
            pltpu.VMEM(((n_fft * W - 1).bit_length(), 8, n_fft * W), jnp.int32),
            pltpu.VMEM((n_chip, 2, 2, SLOTS, W), BF16),
            pltpu.VMEM(beta.shape, BF16),
            pltpu.VMEM((32 * PAD, W), F32),
            pltpu.VMEM((32, SLOTS * W), BF16),
            pltpu.VMEM((nbr * PAD, W), F32),
            pltpu.VMEM((nbr, SLOTS * W), BF16),
            pltpu.VMEM((32, W), F32),
            pltpu.VMEM((8, W), F32),
            pltpu.VMEM((n_fft, 8, W), F32),
            pltpu.VMEM((nbr * PAD, W), F32),
            pltpu.VMEM((n_chip, 4 * SLOTS, W), BF16),
            pltpu.VMEM((n_chip, 4 * SLOTS, W), BF16),
            pltpu.VMEM(psi.shape, F32),
            dma((2,)), dma((2,)), dma((2,)), dma((2,)),
            dma, dma, dma, dma, dma, dma, dma, dma, dma((len(operands),)), dma((2,)),
        ],
        compiler_params=pltpu.CompilerParams(
            collective_id=0, has_side_effects=True, vmem_limit_bytes=56 * 1024 * 1024
        ),
    )(*operands)


def solution(mesh):
    in_specs = (
        P("band", None, "fft", None),
        P(),
        P(),
        P(),
        P("fft", None),
        P("band", None, None, "fft", None),
        P(),
    )
    out_specs = P("band", None, "fft", None)
    part = functools.partial(body, mesh.shape["band"], mesh.shape["fft"])
    return jax.shard_map(part, mesh=mesh, in_specs=in_specs, out_specs=out_specs, check_vma=False)
```

```python
import functools
import math

import jax
import jax.numpy as jnp
import numpy as np
from jax import lax
from jax.experimental import pallas as pl
from jax.experimental.pallas import tpu as pltpu
from jax.sharding import PartitionSpec as P

NG = 240
RAD = 60
W = 128
SLOTS = 80
PLANES = 8
LOW = 64
PAD = 88
F32 = jnp.float32
BF16 = jnp.bfloat16
MESH = pl.DeviceIdType.MESH


def tables():
    wave = np.arange(W) - RAD
    pos = np.arange(256)
    angle = 2.0 * np.pi * ((wave[:, None] * pos[None, :]) % NG) / NG
    inside = (pos < NG)[None, :]
    co, si = np.cos(angle) * inside, np.sin(angle) * inside
    z_re = np.concatenate([co.T, -si.T], axis=1)
    z_im = np.concatenate([si.T, co.T], axis=1)
    y_out = np.block([[co, si], [-si, co]])
    y_back = y_out.T
    cx, sx = co[:, :NG].T, si[:, :NG].T
    x_out = np.block([[cx, -sx], [sx, cx]])
    x_out = x_out.reshape(2, NG // 16, 16, 2, W).transpose(1, 0, 2, 4, 3).reshape(2 * NG, 2 * W)
    x_back = x_out.T
    return [np.asarray(t, np.float32).astype(jnp.bfloat16) for t in (np.stack([z_re, z_im]), y_out, x_out, x_back, y_back)]


def iota(shape, dim):
    return lax.broadcasted_iota(jnp.int32, shape, dim)


def dot(a, b, dims=((1,), (0,)), precision=None):
    return lax.dot_general(a, b, (dims, ((), ())), preferred_element_type=F32, precision=precision)


NT = ((1,), (1,))
TN = ((0,), (0,))


def kernel(
    n_band, n_fft,
    len_h, col_h, plane_h, col2_h, len2_h, psi_h, pot_h, beta_h, coup_h, zt_h, yf_h, xf_h, xb_h, yb_h,
    out_h,
    len_s, col_s, plane_ref, col_ref, len_ref, psi_ref, pot_ref, beta_ref, coup_ref, zt_ref, yf_ref, xf_ref, xb_ref, yb_ref, out_ref,
    lenb, colb, psi2, z_tab, send1, recv1, send2, recv2,
    chi_f, chi_b, yhot, v3, dense, box, boxes, leave, come,
    gath, beta_other, beta_f, beta_t, psi_f, psi_t, product, part_send, part_recv, term_f, term_send, term_recv, base,
    s1, r1, s2, r2, sg, rg, sp, rp, sn, rn, sb, rb, load_sem, out_sem,
):
    f = lax.axis_index("fft")
    g = lax.axis_index("band")
    nb = 2
    tot = n_fft * SLOTS
    nq = 2 * PLANES
    cap = -(-tot // 2 // W) * W

    def others_along_fft(start):
        n_x = n_fft // 8
        steps = [n_x // 2] + [n_x // 2 + sign * d for d in range(1, n_x // 2 + 1) for sign in (-1, 1) if n_x // 2 + sign * d < n_x]
        x, z = f >> 3, f & 7

        @pl.loop(0, 7)
        def _(j):
            half = (j + 1) >> 1
            to_z = (z + 4 + jnp.where((j & 1) == 1, -half, half)) & 7
            for step in steps:
                start((((x + step) & (n_x - 1)) << 3) + to_z)

        for step in steps:
            if step:
                start((((x + step) & (n_x - 1)) << 3) + z)

    barrier = pltpu.get_barrier_semaphore()

    others_along_fft(lambda e: pl.semaphore_signal(barrier, inc=1, device_id={"fft": e}, device_id_type=MESH))

    n_chip = n_band // 2
    chip = lax.div(g, 2)
    other = g + 1 - 2 * lax.rem(g, 2)

    def same_core(k):
        return lax.rem(g + 2 * k, n_band)

    pl.semaphore_signal(barrier, inc=1, device_id={"band": other}, device_id_type=MESH)
    for k in range(1, n_chip):
        pl.semaphore_signal(barrier, inc=1, device_id={"band": same_core(k)}, device_id_type=MESH)

    pairs = (
        (len_h, len_s), (col_h, col_s), (plane_h, plane_ref), (psi_h, psi_ref), (zt_h, zt_ref), (col2_h, col_ref), (len2_h, len_ref), (pot_h, pot_ref),
        (beta_h, beta_ref), (xf_h, xf_ref), (yf_h, yf_ref), (yb_h, yb_ref), (xb_h, xb_ref), (coup_h, coup_ref),
    )
    loads = [pltpu.make_async_copy(far, near, load_sem.at[i]) for i, (far, near) in enumerate(pairs)]
    for load in loads:
        load.start()
    for load in loads[:5]:
        load.wait()

    @pl.loop(0, SLOTS, unroll=8)
    def _(s):
        lenb[pl.ds(s, 1), :] = jnp.full((1, W), len_s[f * SLOTS + s], jnp.int32)
        colb[pl.ds(s, 1), :] = jnp.full((1, W), col_s[f * SLOTS + s], jnp.int32)

    wave_z = iota((SLOTS, W), 1) - RAD
    in_sphere = (2 * jnp.abs(wave_z) < lenb[...]).astype(F32)
    psi2[...] = jnp.zeros(psi2.shape, BF16)
    for b in range(nb):
        for c in range(2):
            psi2[b, 0:SLOTS, c * W:(c + 1) * W] = (psi_ref[b, c].astype(F32) * in_sphere).astype(BF16)

    n_slot = n_fft * PLANES
    hot_z = (iota((256, n_slot), 0) == plane_ref[...]).astype(F32).T.astype(BF16)
    z_re = dot(hot_z, zt_ref[0]).reshape(n_fft, 1, PLANES, 256)
    z_im = dot(hot_z, zt_ref[1]).reshape(n_fft, 1, PLANES, 256)
    z_tab[...] = jnp.concatenate([z_re, z_im], axis=1).reshape(n_fft * nq, 256).astype(BF16)
    for b in range(nb):
        along = dot(z_tab[...], psi2[b], NT)
        send1[b] = along.reshape(n_fft, nq, W).astype(BF16)
        recv1[b, f] = send1[b, f]

    pl.semaphore_wait(barrier, n_fft - 1 + n_chip)

    def exchange(send, recv, send_sem, recv_sem, b):
        def start(e):
            pltpu.make_async_remote_copy(
                src_ref=send.at[b, e], dst_ref=recv.at[b, f], send_sem=send_sem.at[b], recv_sem=recv_sem.at[b],
                device_id={"fft": e}, device_id_type=MESH,
            ).start()

        others_along_fft(start)

    def wait_bytes(ref, sem):
        pltpu.make_async_copy(ref, ref, sem).wait()

    exchange(send1, recv1, s1, r1, 0)

    def to_chips(k, src, dst, send_sem, recv_sem):
        return pltpu.make_async_remote_copy(
            src_ref=src, dst_ref=dst, send_sem=send_sem, recv_sem=recv_sem,
            device_id={"band": same_core(k)}, device_id_type=MESH,
        )

    for k in range(1, n_chip):
        to_chips(k, psi_ref, gath.at[chip], sg, rg).start()
    loads[8].wait()
    swap_beta = pltpu.make_async_remote_copy(
        src_ref=beta_ref, dst_ref=beta_other, send_sem=sb, recv_sem=rb, device_id={"band": other}, device_id_type=MESH
    )
    swap_beta.start()
    gath[chip] = psi_ref[...]

    bits = (n_fft * W - 1).bit_length()
    lane8 = iota((8, W), 1)

    def moved_left(cols, k):
        if k >= 7:
            far = 1 << (k - 7)
            return cols[far:] + [jnp.zeros_like(cols[0])] * min(far, len(cols))
        step = 1 << k
        rolled = [pltpu.roll(col, W - step, 1) for col in cols]
        lane = iota(cols[0].shape, 1)
        return [jnp.where(lane < W - step, one, two) for one, two in zip(rolled, rolled[1:] + [jnp.zeros_like(cols[0])])]

    def moved_right(cols, k):
        if k >= 7:
            far = 1 << (k - 7)
            return [jnp.zeros_like(cols[0])] * min(far, len(cols)) + cols[:max(len(cols) - far, 0)]
        step = 1 << k
        rolled = [pltpu.roll(col, step, 1) for col in cols]
        lane = iota(cols[0].shape, 1)
        return [jnp.where(lane >= step, one, two) for one, two in zip(rolled, [jnp.zeros_like(cols[0])] + rolled[:-1])]

    def place_tables():
        dense = []
        for r in range(tot // W):
            used = jnp.broadcast_to(len_ref[r:r + 1, :], (8, W)) > 0
            dense.append(jnp.where(used, jnp.broadcast_to(col_ref[r:r + 1, :], (8, W)), -1))
        cols, moves = [], []
        ahead = jnp.zeros((8, 1), F32)
        for e in range(n_fft):
            first, off = 80 * e // W, 80 * e % W
            piece = pltpu.roll(dense[first], W - off, 1) if off else dense[first]
            if off + 80 > W:
                piece = jnp.where(lane8 < W - off, piece, pltpu.roll(dense[first + 1], W - off, 1))
            piece = jnp.where(lane8 < 80, piece, -1)
            used = piece >= 0
            cols.append(piece)
            moves.append(jnp.where(used, jnp.broadcast_to(ahead, (8, W)), 0.0).astype(jnp.int32))
            ahead = ahead + (float(W) - jnp.sum(used.astype(F32), axis=1, keepdims=True))
        for k in range(bits):
            next_moves, next_cols = moved_left(moves, k), moved_left(cols, k)
            for e in range(n_fft):
                leaves, comes = (moves[e] >> k) & 1, (next_moves[e] >> k) & 1
                at = slice(e * W, (e + 1) * W)
                leave[k, :, at] = leaves
                come[k, :, at] = comes
                moves[e] = jnp.where(comes > 0, next_moves[e], jnp.where(leaves > 0, 0, moves[e]))
                cols[e] = jnp.where(comes > 0, next_cols[e], jnp.where(leaves > 0, -1, cols[e]))
        for r in range(cap // W):
            at = slice(r * W, (r + 1) * W)
            c, d = cols[r] >> 7, cols[r] & (W - 1)
            chi = (c & (LOW - 1)).astype(F32)
            chi_f[:, at] = chi
            chi_b[:, at] = jnp.concatenate([chi, chi], axis=0).astype(BF16)
            row = jnp.where(cols[r] < 0, -1, (c >> 6) * W + d)
            yhot[:, at] = (iota((2 * W, W), 0) == row[:1]).astype(F32).astype(BF16)

    def diagonal():
        gx, gy = colb[...] // W - RAD, colb[...] % W - RAD
        kinetic = (gx * gx + gy * gy + wave_z * wave_z).astype(F32) / float(RAD * RAD)
        for b in range(nb):
            for c in range(2):
                base[b, c] = kinetic * in_sphere * psi_ref[b, c].astype(F32)

    def potential_rows():
        @pl.loop(0, NG // 24)
        def _(m3):
            for u in range(3):
                m = m3 * 3 + u
                for r in range(8):
                    start = 240 * r
                    low = start // W * W
                    width = 256 if start - low <= 16 else 384
                    piece = pot_ref[:, pl.ds(pl.multiple_of(m * 1920 + low, W), width)]
                    if start - low:
                        piece = pltpu.roll(piece, width - (start - low), 1)
                    for c in range(2):
                        v3[c, pl.ds(pl.multiple_of((m * 8 + r) * 8, 8), 8), :] = piece[:, c * W:(c + 1) * W]

    def projector_rows():
        swap_beta.wait_recv()
        for a, source in enumerate((beta_ref, beta_other)):
            for k in range(8):
                for c in range(2):
                    beta_f[pl.ds((c * 16 + a * 8 + k) * PAD, SLOTS), :] = source[0, k, c].astype(F32) * in_sphere

        @pl.loop(0, SLOTS // 4)
        def _(s4):
            for u in range(4):
                s = s4 * 4 + u
                rows = beta_f[pl.ds(s, 32, stride=PAD), :]
                beta_t[:, pl.ds(pl.multiple_of(s * W, W), W)] = rows.astype(BF16)

    def to_planes(b):
        wait_bytes(recv1.at[b, pl.ds(0, n_fft - 1)], r1.at[b])

    def both(mask):
        return jnp.concatenate([mask, mask], axis=0)

    def pack_sticks(b):
        cols = [recv1[b, e].astype(F32) for e in range(n_fft)]
        for k in range(bits):
            arriving = moved_left(cols, k)
            cols = [jnp.where(both(come[k, :, e * W:(e + 1) * W]) > 0, arriving[e], cols[e]) for e in range(n_fft)]
        dense[...] = jnp.concatenate(cols[:cap // W], axis=1).astype(BF16)

    def place_columns(b):
        sticks, place = dense[...], chi_b[...]
        rows = [jnp.where(place == jnp.asarray(i, BF16), sticks, jnp.asarray(0, BF16)) for i in range(LOW)]
        placed = dot(jnp.concatenate(rows, axis=0), yhot[...], NT)
        for h in range(2):
            box[h] = placed[:, h * W:(h + 1) * W]

    def transform():
        @pl.loop(0, PLANES // 4)
        def _(quad):
            along_x = []
            for p in range(2):
                pair = []
                for u in range(2):
                    t = quad * 4 + p * 2 + u
                    pair.append(jnp.concatenate([box[h, pl.ds(t, W, stride=PLANES), :] for h in range(2)], axis=0))
                wide = dot(xf_ref[...], jnp.concatenate(pair, axis=1).astype(BF16)).astype(BF16)
                wide = wide.reshape(NG // 16, 2, 16, 2 * W)
                for u in range(2):
                    part = [wide[:, c, :, u * W:(u + 1) * W].reshape(NG, W) for c in range(2)]
                    along_x.append(jnp.concatenate(part, axis=1))
            full = dot(jnp.concatenate(along_x, axis=0), yf_ref[...])
            weighted = []
            for u in range(4):
                weight = [v3[c, pl.ds(quad * 4 + u, NG, stride=PLANES), :] for c in range(2)]
                weighted.append((full[u * NG:(u + 1) * NG] * jnp.concatenate(weight * 2, axis=1)).astype(BF16))
            back = dot(jnp.concatenate(weighted, axis=0), yb_ref[...]).astype(BF16)
            for p in range(2):
                pair = [back[(p * 2 + u) * NG:(p * 2 + u + 1) * NG] for u in range(2)]
                pair = [part.reshape(NG // 16, 1, 16, 2 * W) for part in pair]
                pair = [jnp.concatenate([part[..., :W], part[..., W:]], axis=1).reshape(2 * NG, W) for part in pair]
                wide = dot(xb_ref[...], jnp.concatenate(pair, axis=1))
                for u in range(2):
                    t = quad * 4 + p * 2 + u
                    for h in range(2):
                        box[h, pl.ds(t, W, stride=PLANES), :] = wide[h * W:(h + 1) * W, u * W:(u + 1) * W]

    def to_sticks(b):
        boxes[...] = jnp.concatenate([box[0], box[1]], axis=1).astype(BF16)

        rows = dot(boxes[...], yhot[...])
        place = both(chi_f[...])
        found = jnp.zeros((nq, cap), F32)
        for i in range(LOW):
            found = jnp.where(place == float(i), rows[i * nq:(i + 1) * nq], found)
        cols = [found[:, r * W:(r + 1) * W] for r in range(cap // W)]
        cols = cols + [jnp.zeros((nq, W), F32)] * (n_fft - len(cols))
        for k in reversed(range(bits)):
            leaving = moved_right(cols, k)
            cols = [jnp.where(both(leave[k, :, e * W:(e + 1) * W]) > 0, leaving[e], cols[e]) for e in range(n_fft)]
        for e in range(n_fft):
            send2[b, e] = cols[e].astype(BF16)
        recv2[b, f] = send2[b, f]
        exchange(send2, recv2, s2, r2, b)

    nbr = 2 * nb * n_chip

    def cross(x):
        return jnp.where(iota(x.shape, 1) % 2 == 0, pltpu.roll(x, W - 1, 1), -pltpu.roll(x, 1, 1))

    def project():
        if n_chip > 1:
            wait_bytes(gath.at[pl.ds(0, n_chip - 1)], rg)

        @pl.loop(0, n_chip)
        def _(h):
            for b in range(nb):
                for c in range(2):
                    psi_f[pl.ds(pl.multiple_of((h * 4 + b * 2 + c) * PAD, 8), SLOTS), :] = gath[h, b, c].astype(F32)

        @pl.loop(0, SLOTS // 8)
        def _(s8):
            for u in range(8):
                s = s8 * 8 + u
                psi_t[:, pl.ds(pl.multiple_of(s * W, W), W)] = psi_f[pl.ds(s, nbr, stride=PAD), :].astype(BF16)

        product[...] = jnp.zeros(product.shape, F32)
        product[:, :nbr] = dot(beta_t[...], psi_t[...], NT)
        one, two = [product[a * 8:a * 8 + 8] + cross(product[16 + a * 8:24 + a * 8]) for a in range(2)]
        part_send[...] = jnp.where(lane8 < nbr, one, pltpu.roll(two, nbr, 1))
        part_recv[f] = part_send[...]

        @pl.loop(1, n_fft)
        def _(k):
            pltpu.make_async_remote_copy(
                src_ref=part_send, dst_ref=part_recv.at[f], send_sem=sp, recv_sem=rp,
                device_id={"fft": lax.rem(f + k, n_fft)}, device_id_type=MESH,
            ).start()

    def expand():
        wait_bytes(part_recv.at[pl.ds(0, n_fft - 1)], rp)
        whole = jnp.sum(part_recv[...], axis=0)
        coupling = jnp.concatenate([coup_ref[g], coup_ref[other]], axis=0)
        coupled = dot(coupling, whole, precision=lax.Precision.HIGHEST)
        coeffs = jnp.where(lane8 < nbr, coupled[:8], coupled[8:]).astype(BF16).astype(F32)
        crossed = -cross(coeffs)
        factors = [x if a == 0 else pltpu.roll(x, W - nbr, 1) for x in (coeffs, crossed) for a in range(2)]
        factors = jnp.concatenate(factors + [jnp.zeros((W - 32, W), F32)], axis=0).T[:nbr, :32].astype(BF16)

        @pl.loop(0, SLOTS // 16)
        def _(m):
            terms = dot(factors, beta_t[:, pl.ds(pl.multiple_of(m * 2048, 2048), 2048)])
            for i in range(16):
                term_f[pl.ds(m * 16 + i, nbr, stride=PAD), :] = terms[:, i * W:(i + 1) * W]

        for k in reversed(range(n_chip)):
            h = lax.div(same_core(k), 2)
            for i in range(4):
                at = pl.ds(pl.multiple_of((h * 4 + i) * PAD, 8), SLOTS)
                term_send[h, i * SLOTS:(i + 1) * SLOTS, :] = term_f[at, :].astype(BF16)
            if k:
                to_chips(k, term_send.at[h], term_recv.at[chip], sn, rn).start()
            else:
                term_recv[chip] = term_send[chip]

    for load in loads[5:8] + loads[9:]:
        load.wait()
    diagonal()
    place_tables()
    exchange(send1, recv1, s1, r1, 1)
    potential_rows()
    projector_rows()
    to_planes(0)
    pack_sticks(0)
    place_columns(0)
    project()
    transform()
    to_sticks(0)
    to_planes(1)
    pack_sticks(1)
    place_columns(1)
    transform()
    expand()
    to_sticks(1)

    if n_chip > 1:
        wait_bytes(term_recv.at[pl.ds(0, n_chip - 1)], rn)
    for b in range(nb):
        for c in range(2):
            at = pl.ds((b * 2 + c) * SLOTS, SLOTS)
            nonlocal_sum = term_recv[0, at, :].astype(F32)
            for h in range(1, n_chip):
                nonlocal_sum = nonlocal_sum + term_recv[h, at, :].astype(F32)
            base[b, c] = base[b, c] + in_sphere * nonlocal_sum

    stores = [pltpu.make_async_copy(out_ref.at[b], out_h.at[b], out_sem.at[b]) for b in range(nb)]
    for b in range(nb):
        wait_bytes(recv2.at[b, pl.ds(0, n_fft - 1)], r2.at[b])
        local = dot(recv2[b].reshape(n_fft * nq, W), z_tab[...], TN) * (1.0 / float(NG**3))
        for c in range(2):
            out_ref[b, c] = base[b, c] + in_sphere * local[:SLOTS, c * W:(c + 1) * W]
        stores[b].start()

    for b in range(nb):
        wait_bytes(send1.at[b, pl.ds(0, n_fft - 1)], s1.at[b])
        wait_bytes(send2.at[b, pl.ds(0, n_fft - 1)], s2.at[b])
    if n_chip > 1:
        wait_bytes(gath.at[pl.ds(0, n_chip - 1)], sg)
        wait_bytes(term_send.at[pl.ds(0, n_chip - 1)], sn)
    wait_bytes(part_recv.at[pl.ds(0, n_fft - 1)], sp)
    swap_beta.wait_send()
    for b in range(nb):
        stores[b].wait()


def body(n_band, n_fft, psi, stick_col, stick_len, plane_z, potential, beta, coupling):
    tot = n_fft * SLOTS
    n_slot = n_fft * PLANES
    nq = 2 * PLANES
    n_chip = n_band // 2
    nbr = 4 * n_chip
    cap = -(-tot // 2 // W) * W
    consts = [jnp.asarray(t) for t in tables()]
    hbm = pl.BlockSpec(memory_space=pl.ANY)
    dma = pltpu.SemaphoreType.DMA
    operands = [
        stick_len, stick_col, plane_z.reshape(1, n_slot), stick_col.reshape(tot // W, W), stick_len.reshape(tot // W, W),
        psi, potential, beta, coupling, *consts,
    ]
    return pl.pallas_call(
        functools.partial(kernel, n_band, n_fft),
        out_shape=jax.ShapeDtypeStruct(psi.shape, F32),
        in_specs=[hbm] * len(operands),
        out_specs=hbm,
        scratch_shapes=[
            *[(pltpu.SMEM if i < 2 else pltpu.VMEM)(x.shape, x.dtype) for i, x in enumerate(operands)],
            pltpu.VMEM(psi.shape, F32),
            pltpu.VMEM((SLOTS, W), jnp.int32),
            pltpu.VMEM((SLOTS, W), jnp.int32),
            pltpu.VMEM((2, W, 2 * W), BF16),
            pltpu.VMEM((n_fft * nq, 2 * W), BF16),
            pltpu.VMEM((2, n_fft, nq, W), BF16),
            pltpu.VMEM((2, n_fft, nq, W), BF16),
            pltpu.VMEM((2, n_fft, nq, W), BF16),
            pltpu.VMEM((2, n_fft, nq, W), BF16),
            pltpu.VMEM((8, cap), F32),
            pltpu.VMEM((nq, cap), BF16),
            pltpu.VMEM((2 * W, cap), BF16),
            pltpu.VMEM((2, NG * PLANES, W), F32),
            pltpu.VMEM((nq, cap), BF16),
            pltpu.VMEM((2, LOW * nq, W), F32),
            pltpu.VMEM((LOW * nq, 2 * W), BF16),
            pltpu.VMEM(((n_fft * W - 1).bit_length(), 8, n_fft * W), jnp.int32),
            pltpu.VMEM(((n_fft * W - 1).bit_length(), 8, n_fft * W), jnp.int32),
            pltpu.VMEM((n_chip, 2, 2, SLOTS, W), BF16),
            pltpu.VMEM(beta.shape, BF16),
            pltpu.VMEM((32 * PAD, W), F32),
            pltpu.VMEM((32, SLOTS * W), BF16),
            pltpu.VMEM((nbr * PAD, W), F32),
            pltpu.VMEM((nbr, SLOTS * W), BF16),
            pltpu.VMEM((32, W), F32),
            pltpu.VMEM((8, W), F32),
            pltpu.VMEM((n_fft, 8, W), F32),
            pltpu.VMEM((nbr * PAD, W), F32),
            pltpu.VMEM((n_chip, 4 * SLOTS, W), BF16),
            pltpu.VMEM((n_chip, 4 * SLOTS, W), BF16),
            pltpu.VMEM(psi.shape, F32),
            dma((2,)), dma((2,)), dma((2,)), dma((2,)),
            dma, dma, dma, dma, dma, dma, dma, dma, dma((len(operands),)), dma((2,)),
        ],
        compiler_params=pltpu.CompilerParams(
            collective_id=0, has_side_effects=True, vmem_limit_bytes=56 * 1024 * 1024
        ),
    )(*operands)


def solution(mesh):
    in_specs = (
        P("band", None, "fft", None),
        P(),
        P(),
        P(),
        P("fft", None),
        P("band", None, None, "fft", None),
        P(),
    )
    out_specs = P("band", None, "fft", None)
    part = functools.partial(body, mesh.shape["band"], mesh.shape["fft"])
    return jax.shard_map(part, mesh=mesh, in_specs=in_specs, out_specs=out_specs, check_vma=False)
```

```python
import functools
import math

import jax
import jax.numpy as jnp
import numpy as np
from jax import lax
from jax.experimental import pallas as pl
from jax.experimental.pallas import tpu as pltpu
from jax.sharding import PartitionSpec as P

NG = 240
RAD = 60
W = 128
SLOTS = 80
PLANES = 8
LOW = 64
PAD = 88
F32 = jnp.float32
BF16 = jnp.bfloat16
MESH = pl.DeviceIdType.MESH


def tables():
    wave = np.arange(W) - RAD
    pos = np.arange(256)
    angle = 2.0 * np.pi * ((wave[:, None] * pos[None, :]) % NG) / NG
    inside = (pos < NG)[None, :]
    co, si = np.cos(angle) * inside, np.sin(angle) * inside
    z_re = np.concatenate([co.T, -si.T], axis=1)
    z_im = np.concatenate([si.T, co.T], axis=1)
    y_out = np.block([[co, si], [-si, co]])
    y_back = y_out.T
    cx, sx = co[:, :NG].T, si[:, :NG].T
    x_out = np.block([[cx, -sx], [sx, cx]])
    x_out = x_out.reshape(2, NG // 16, 16, 2, W).transpose(1, 0, 2, 4, 3).reshape(2 * NG, 2 * W)
    x_back = x_out.T
    return [np.asarray(t, np.float32).astype(jnp.bfloat16) for t in (np.stack([z_re, z_im]), y_out, x_out, x_back, y_back)]


def iota(shape, dim):
    return lax.broadcasted_iota(jnp.int32, shape, dim)


def dot(a, b, dims=((1,), (0,)), precision=None):
    return lax.dot_general(a, b, (dims, ((), ())), preferred_element_type=F32, precision=precision)


NT = ((1,), (1,))
TN = ((0,), (0,))


def kernel(
    n_band, n_fft,
    len_h, col_h, plane_h, col2_h, len2_h, psi_h, pot_h, beta_h, coup_h, zt_h, yf_h, xf_h, xb_h, yb_h,
    out_h,
    len_s, col_s, plane_ref, col_ref, len_ref, psi_ref, pot_ref, beta_ref, coup_ref, zt_ref, yf_ref, xf_ref, xb_ref, yb_ref, out_ref,
    lenb, colb, psi2, z_tab, send1, recv1, send2, recv2,
    chi_f, chi_b, yhot, v3, dense, box, boxes, leave, come,
    gath, beta_other, beta_f, beta_t, psi_f, psi_t, product, part_send, part_recv, term_f, term_send, term_recv, base,
    s1, r1, s2, r2, sg, rg, sp, rp, sn, rn, sb, rb, load_sem, out_sem,
):
    f = lax.axis_index("fft")
    g = lax.axis_index("band")
    nb = 2
    tot = n_fft * SLOTS
    nq = 2 * PLANES
    cap = -(-tot // 2 // W) * W

    def others_along_fft(start):
        n_x = n_fft // 8
        steps = [n_x // 2] + [n_x // 2 + sign * d for d in range(1, n_x // 2 + 1) for sign in (-1, 1) if n_x // 2 + sign * d < n_x]
        x, z = f >> 3, f & 7

        @pl.loop(0, 7)
        def _(j):
            half = (j + 1) >> 1
            to_z = (z + 4 + jnp.where((j & 1) == 1, -half, half)) & 7
            for step in steps:
                start((((x + step) & (n_x - 1)) << 3) + to_z)

        for step in steps:
            if step:
                start((((x + step) & (n_x - 1)) << 3) + z)

    barrier = pltpu.get_barrier_semaphore()

    others_along_fft(lambda e: pl.semaphore_signal(barrier, inc=1, device_id={"fft": e}, device_id_type=MESH))

    n_chip = n_band // 2
    chip = lax.div(g, 2)
    other = g + 1 - 2 * lax.rem(g, 2)

    def same_core(k):
        return lax.rem(g + 2 * k, n_band)

    pl.semaphore_signal(barrier, inc=1, device_id={"band": other}, device_id_type=MESH)
    for k in range(1, n_chip):
        pl.semaphore_signal(barrier, inc=1, device_id={"band": same_core(k)}, device_id_type=MESH)

    pairs = (
        (len_h, len_s), (col_h, col_s), (plane_h, plane_ref), (psi_h, psi_ref), (zt_h, zt_ref), (col2_h, col_ref), (len2_h, len_ref), (pot_h, pot_ref),
        (beta_h, beta_ref), (xf_h, xf_ref), (yf_h, yf_ref), (yb_h, yb_ref), (xb_h, xb_ref), (coup_h, coup_ref),
    )
    loads = [pltpu.make_async_copy(far, near, load_sem.at[i]) for i, (far, near) in enumerate(pairs)]
    for load in loads:
        load.start()
    for load in loads[:5]:
        load.wait()

    @pl.loop(0, SLOTS, unroll=8)
    def _(s):
        lenb[pl.ds(s, 1), :] = jnp.full((1, W), len_s[f * SLOTS + s], jnp.int32)
        colb[pl.ds(s, 1), :] = jnp.full((1, W), col_s[f * SLOTS + s], jnp.int32)

    wave_z = iota((SLOTS, W), 1) - RAD
    in_sphere = (2 * jnp.abs(wave_z) < lenb[...]).astype(F32)
    psi2[...] = jnp.zeros(psi2.shape, BF16)
    for b in range(nb):
        for c in range(2):
            psi2[b, 0:SLOTS, c * W:(c + 1) * W] = (psi_ref[b, c].astype(F32) * in_sphere).astype(BF16)

    n_slot = n_fft * PLANES
    hot_z = (iota((256, n_slot), 0) == plane_ref[...]).astype(F32).T.astype(BF16)
    z_re = dot(hot_z, zt_ref[0]).reshape(n_fft, 1, PLANES, 256)
    z_im = dot(hot_z, zt_ref[1]).reshape(n_fft, 1, PLANES, 256)
    z_tab[...] = jnp.concatenate([z_re, z_im], axis=1).reshape(n_fft * nq, 256).astype(BF16)
    for b in range(nb):
        along = dot(z_tab[...], psi2[b], NT)
        send1[b] = along.reshape(n_fft, nq, W).astype(BF16)
        recv1[b, f] = send1[b, f]

    pl.semaphore_wait(barrier, n_fft - 1 + n_chip)

    def exchange(send, recv, send_sem, recv_sem, b):
        def start(e):
            pltpu.make_async_remote_copy(
                src_ref=send.at[b, e], dst_ref=recv.at[b, f], send_sem=send_sem.at[b], recv_sem=recv_sem.at[b],
                device_id={"fft": e}, device_id_type=MESH,
            ).start()

        others_along_fft(start)

    def wait_bytes(ref, sem):
        pltpu.make_async_copy(ref, ref, sem).wait()

    exchange(send1, recv1, s1, r1, 0)

    def to_chips(k, src, dst, send_sem, recv_sem):
        return pltpu.make_async_remote_copy(
            src_ref=src, dst_ref=dst, send_sem=send_sem, recv_sem=recv_sem,
            device_id={"band": same_core(k)}, device_id_type=MESH,
        )

    for k in range(1, n_chip):
        to_chips(k, psi_ref, gath.at[chip], sg, rg).start()
    loads[8].wait()
    swap_beta = pltpu.make_async_remote_copy(
        src_ref=beta_ref, dst_ref=beta_other, send_sem=sb, recv_sem=rb, device_id={"band": other}, device_id_type=MESH
    )
    swap_beta.start()
    gath[chip] = psi_ref[...]

    bits = (n_fft * W - 1).bit_length()
    lane8 = iota((8, W), 1)

    def moved_left(cols, k):
        if k >= 7:
            far = 1 << (k - 7)
            return cols[far:] + [jnp.zeros_like(cols[0])] * min(far, len(cols))
        step = 1 << k
        rolled = [pltpu.roll(col, W - step, 1) for col in cols]
        lane = iota(cols[0].shape, 1)
        return [jnp.where(lane < W - step, one, two) for one, two in zip(rolled, rolled[1:] + [jnp.zeros_like(cols[0])])]

    def moved_right(cols, k):
        if k >= 7:
            far = 1 << (k - 7)
            return [jnp.zeros_like(cols[0])] * min(far, len(cols)) + cols[:max(len(cols) - far, 0)]
        step = 1 << k
        rolled = [pltpu.roll(col, step, 1) for col in cols]
        lane = iota(cols[0].shape, 1)
        return [jnp.where(lane >= step, one, two) for one, two in zip(rolled, [jnp.zeros_like(cols[0])] + rolled[:-1])]

    def place_tables():
        dense = []
        for r in range(tot // W):
            used = jnp.broadcast_to(len_ref[r:r + 1, :], (8, W)) > 0
            dense.append(jnp.where(used, jnp.broadcast_to(col_ref[r:r + 1, :], (8, W)), -1))
        cols, moves = [], []
        ahead = jnp.zeros((8, 1), F32)
        for e in range(n_fft):
            first, off = 80 * e // W, 80 * e % W
            piece = pltpu.roll(dense[first], W - off, 1) if off else dense[first]
            if off + 80 > W:
                piece = jnp.where(lane8 < W - off, piece, pltpu.roll(dense[first + 1], W - off, 1))
            piece = jnp.where(lane8 < 80, piece, -1)
            used = piece >= 0
            cols.append(piece)
            moves.append(jnp.where(used, jnp.broadcast_to(ahead, (8, W)), 0.0).astype(jnp.int32))
            ahead = ahead + (float(W) - jnp.sum(used.astype(F32), axis=1, keepdims=True))
        for k in range(bits):
            next_moves, next_cols = moved_left(moves, k), moved_left(cols, k)
            for e in range(n_fft):
                leaves, comes = (moves[e] >> k) & 1, (next_moves[e] >> k) & 1
                at = slice(e * W, (e + 1) * W)
                leave[k, :, at] = leaves
                come[k, :, at] = comes
                moves[e] = jnp.where(comes > 0, next_moves[e], jnp.where(leaves > 0, 0, moves[e]))
                cols[e] = jnp.where(comes > 0, next_cols[e], jnp.where(leaves > 0, -1, cols[e]))
        for r in range(cap // W):
            at = slice(r * W, (r + 1) * W)
            c, d = cols[r] >> 7, cols[r] & (W - 1)
            chi = (c & (LOW - 1)).astype(F32)
            chi_f[:, at] = chi
            chi_b[:, at] = jnp.concatenate([chi, chi], axis=0).astype(BF16)
            row = jnp.where(cols[r] < 0, -1, (c >> 6) * W + d)
            yhot[:, at] = (iota((2 * W, W), 0) == row[:1]).astype(F32).astype(BF16)

    def diagonal():
        gx, gy = colb[...] // W - RAD, colb[...] % W - RAD
        kinetic = (gx * gx + gy * gy + wave_z * wave_z).astype(F32) / float(RAD * RAD)
        for b in range(nb):
            for c in range(2):
                base[b, c] = kinetic * in_sphere * psi_ref[b, c].astype(F32)

    def potential_rows():
        @pl.loop(0, NG // 24)
        def _(m3):
            for u in range(3):
                m = m3 * 3 + u
                for r in range(8):
                    start = 240 * r
                    low = start // W * W
                    width = 256 if start - low <= 16 else 384
                    piece = pot_ref[:, pl.ds(pl.multiple_of(m * 1920 + low, W), width)]
                    if start - low:
                        piece = pltpu.roll(piece, width - (start - low), 1)
                    for c in range(2):
                        v3[c, pl.ds(pl.multiple_of((m * 8 + r) * 8, 8), 8), :] = piece[:, c * W:(c + 1) * W]

    def projector_rows():
        swap_beta.wait_recv()
        for a, source in enumerate((beta_ref, beta_other)):
            for k in range(8):
                for c in range(2):
                    beta_f[pl.ds((c * 16 + a * 8 + k) * PAD, SLOTS), :] = source[0, k, c].astype(F32) * in_sphere

        @pl.loop(0, SLOTS // 4)
        def _(s4):
            for u in range(4):
                s = s4 * 4 + u
                rows = beta_f[pl.ds(s, 32, stride=PAD), :]
                beta_t[:, pl.ds(pl.multiple_of(s * W, W), W)] = rows.astype(BF16)

    def to_planes(b):
        wait_bytes(recv1.at[b, pl.ds(0, n_fft - 1)], r1.at[b])

    def both(mask):
        return jnp.concatenate([mask, mask], axis=0)

    def pack_sticks(b):
        cols = [recv1[b, e].astype(F32) for e in range(n_fft)]
        for k in range(bits):
            arriving = moved_left(cols, k)
            cols = [jnp.where(both(come[k, :, e * W:(e + 1) * W]) > 0, arriving[e], cols[e]) for e in range(n_fft)]
        dense[...] = jnp.concatenate(cols[:cap // W], axis=1).astype(BF16)

    def place_columns(b):
        sticks, place = dense[...], chi_b[...]
        rows = [jnp.where(place == jnp.asarray(i, BF16), sticks, jnp.asarray(0, BF16)) for i in range(LOW)]
        placed = dot(jnp.concatenate(rows, axis=0), yhot[...], NT)
        for h in range(2):
            box[h] = placed[:, h * W:(h + 1) * W]

    def transform():
        @pl.loop(0, PLANES // 4)
        def _(quad):
            along_x = []
            for p in range(2):
                pair = []
                for u in range(2):
                    t = quad * 4 + p * 2 + u
                    pair.append(jnp.concatenate([box[h, pl.ds(t, W, stride=PLANES), :] for h in range(2)], axis=0))
                wide = dot(xf_ref[...], jnp.concatenate(pair, axis=1).astype(BF16)).astype(BF16)
                wide = wide.reshape(NG // 16, 2, 16, 2 * W)
                for u in range(2):
                    part = [wide[:, c, :, u * W:(u + 1) * W].reshape(NG, W) for c in range(2)]
                    along_x.append(jnp.concatenate(part, axis=1))
            full = dot(jnp.concatenate(along_x, axis=0), yf_ref[...])
            weighted = []
            for u in range(4):
                weight = [v3[c, pl.ds(quad * 4 + u, NG, stride=PLANES), :] for c in range(2)]
                weighted.append((full[u * NG:(u + 1) * NG] * jnp.concatenate(weight * 2, axis=1)).astype(BF16))
            back = dot(jnp.concatenate(weighted, axis=0), yb_ref[...]).astype(BF16)
            for p in range(2):
                pair = [back[(p * 2 + u) * NG:(p * 2 + u + 1) * NG] for u in range(2)]
                pair = [part.reshape(NG // 16, 1, 16, 2 * W) for part in pair]
                pair = [jnp.concatenate([part[..., :W], part[..., W:]], axis=1).reshape(2 * NG, W) for part in pair]
                wide = dot(xb_ref[...], jnp.concatenate(pair, axis=1))
                for u in range(2):
                    t = quad * 4 + p * 2 + u
                    for h in range(2):
                        box[h, pl.ds(t, W, stride=PLANES), :] = wide[h * W:(h + 1) * W, u * W:(u + 1) * W]

    def to_sticks(b, beside=None, after=None):
        boxes[...] = jnp.concatenate([box[0], box[1]], axis=1).astype(BF16)

        if beside is not None:
            beside()
        rows = dot(boxes[...], yhot[...])
        place = both(chi_f[...])
        found = jnp.zeros((nq, cap), F32)
        for i in range(LOW):
            found = jnp.where(place == float(i), rows[i * nq:(i + 1) * nq], found)
        cols = [found[:, r * W:(r + 1) * W] for r in range(cap // W)]
        cols = cols + [jnp.zeros((nq, W), F32)] * (n_fft - len(cols))
        for k in reversed(range(bits)):
            leaving = moved_right(cols, k)
            cols = [jnp.where(both(leave[k, :, e * W:(e + 1) * W]) > 0, leaving[e], cols[e]) for e in range(n_fft)]
        for e in range(n_fft):
            send2[b, e] = cols[e].astype(BF16)
        if after is not None:
            after()
        recv2[b, f] = send2[b, f]
        exchange(send2, recv2, s2, r2, b)

    nbr = 2 * nb * n_chip

    def cross(x):
        return jnp.where(iota(x.shape, 1) % 2 == 0, pltpu.roll(x, W - 1, 1), -pltpu.roll(x, 1, 1))

    def psi_rows():
        if n_chip > 1:
            wait_bytes(gath.at[pl.ds(0, n_chip - 1)], rg)
        for h in range(n_chip):
            for b in range(nb):
                for c in range(2):
                    psi_f[pl.ds((h * 4 + b * 2 + c) * PAD, SLOTS), :] = gath[h, b, c].astype(F32)
        for s in range(SLOTS):
            psi_t[:, s * W:(s + 1) * W] = psi_f[pl.ds(s, nbr, stride=PAD), :].astype(BF16)

    def project():
        product[...] = jnp.zeros(product.shape, F32)
        product[:, :nbr] = dot(beta_t[...], psi_t[...], NT)
        one, two = [product[a * 8:a * 8 + 8] + cross(product[16 + a * 8:24 + a * 8]) for a in range(2)]
        part_send[...] = jnp.where(lane8 < nbr, one, pltpu.roll(two, nbr, 1))
        part_recv[f] = part_send[...]

        @pl.loop(1, n_fft)
        def _(k):
            pltpu.make_async_remote_copy(
                src_ref=part_send, dst_ref=part_recv.at[f], send_sem=sp, recv_sem=rp,
                device_id={"fft": lax.rem(f + k, n_fft)}, device_id_type=MESH,
            ).start()

    def term_factors():
        wait_bytes(part_recv.at[pl.ds(0, n_fft - 1)], rp)
        whole = jnp.sum(part_recv[...], axis=0)
        coupling = jnp.concatenate([coup_ref[g], coup_ref[other]], axis=0)
        coupled = dot(coupling, whole, precision=lax.Precision.HIGHEST)
        coeffs = jnp.where(lane8 < nbr, coupled[:8], coupled[8:]).astype(BF16).astype(F32)
        crossed = -cross(coeffs)
        factors = [x if a == 0 else pltpu.roll(x, W - nbr, 1) for x in (coeffs, crossed) for a in range(2)]
        factors = jnp.concatenate(factors + [jnp.zeros((W - 32, W), F32)], axis=0).T[:nbr, :32].astype(BF16)

        return factors

    def expand_rows(factors):
        for m in range(SLOTS // 16):
            terms = dot(factors, beta_t[:, m * 2048:(m + 1) * 2048])
            for i in range(16):
                term_f[pl.ds(m * 16 + i, nbr, stride=PAD), :] = terms[:, i * W:(i + 1) * W]

    def send_terms():
        for k in reversed(range(n_chip)):
            h = lax.div(same_core(k), 2)
            for i in range(4):
                at = pl.ds(pl.multiple_of((h * 4 + i) * PAD, 8), SLOTS)
                term_send[h, i * SLOTS:(i + 1) * SLOTS, :] = term_f[at, :].astype(BF16)
            if k:
                to_chips(k, term_send.at[h], term_recv.at[chip], sn, rn).start()
            else:
                term_recv[chip] = term_send[chip]

    for load in loads[5:8] + loads[9:]:
        load.wait()
    diagonal()
    place_tables()
    exchange(send1, recv1, s1, r1, 1)
    potential_rows()
    projector_rows()
    to_planes(0)
    psi_rows()
    pack_sticks(0)
    place_columns(0)
    project()
    transform()
    to_planes(1)

    def next_band():
        pack_sticks(1)
        place_columns(1)

    to_sticks(0, after=next_band)
    transform()
    factors = term_factors()
    to_sticks(1, lambda: expand_rows(factors))
    send_terms()

    def local_term(b):
        wait_bytes(recv2.at[b, pl.ds(0, n_fft - 1)], r2.at[b])
        local = dot(recv2[b].reshape(n_fft * nq, W), z_tab[...], TN) * (1.0 / float(NG**3))
        return [in_sphere * local[:SLOTS, c * W:(c + 1) * W] for c in range(2)]

    first = local_term(0)
    for c in range(2):
        out_ref[0, c] = base[0, c] + first[c]
    if n_chip > 1:
        wait_bytes(term_recv.at[pl.ds(0, n_chip - 1)], rn)
    stores = [pltpu.make_async_copy(out_ref.at[b], out_h.at[b], out_sem.at[b]) for b in range(nb)]
    for b in range(nb):
        for c in range(2):
            at = pl.ds((b * 2 + c) * SLOTS, SLOTS)
            nonlocal_sum = term_recv[0, at, :].astype(F32)
            for h in range(1, n_chip):
                nonlocal_sum = nonlocal_sum + term_recv[h, at, :].astype(F32)
            if b == 0:
                out_ref[b, c] = out_ref[b, c] + in_sphere * nonlocal_sum
            else:
                base[b, c] = base[b, c] + in_sphere * nonlocal_sum
        if b == 0:
            stores[b].start()
    second = local_term(1)
    for c in range(2):
        out_ref[1, c] = base[1, c] + second[c]
    stores[1].start()

    for b in range(nb):
        wait_bytes(send1.at[b, pl.ds(0, n_fft - 1)], s1.at[b])
        wait_bytes(send2.at[b, pl.ds(0, n_fft - 1)], s2.at[b])
    if n_chip > 1:
        wait_bytes(gath.at[pl.ds(0, n_chip - 1)], sg)
        wait_bytes(term_send.at[pl.ds(0, n_chip - 1)], sn)
    wait_bytes(part_recv.at[pl.ds(0, n_fft - 1)], sp)
    swap_beta.wait_send()
    for b in range(nb):
        stores[b].wait()


def body(n_band, n_fft, psi, stick_col, stick_len, plane_z, potential, beta, coupling):
    tot = n_fft * SLOTS
    n_slot = n_fft * PLANES
    nq = 2 * PLANES
    n_chip = n_band // 2
    nbr = 4 * n_chip
    cap = -(-tot // 2 // W) * W
    consts = [jnp.asarray(t) for t in tables()]
    hbm = pl.BlockSpec(memory_space=pl.ANY)
    dma = pltpu.SemaphoreType.DMA
    operands = [
        stick_len, stick_col, plane_z.reshape(1, n_slot), stick_col.reshape(tot // W, W), stick_len.reshape(tot // W, W),
        psi, potential, beta, coupling, *consts,
    ]
    return pl.pallas_call(
        functools.partial(kernel, n_band, n_fft),
        out_shape=jax.ShapeDtypeStruct(psi.shape, F32),
        in_specs=[hbm] * len(operands),
        out_specs=hbm,
        scratch_shapes=[
            *[(pltpu.SMEM if i < 2 else pltpu.VMEM)(x.shape, x.dtype) for i, x in enumerate(operands)],
            pltpu.VMEM(psi.shape, F32),
            pltpu.VMEM((SLOTS, W), jnp.int32),
            pltpu.VMEM((SLOTS, W), jnp.int32),
            pltpu.VMEM((2, W, 2 * W), BF16),
            pltpu.VMEM((n_fft * nq, 2 * W), BF16),
            pltpu.VMEM((2, n_fft, nq, W), BF16),
            pltpu.VMEM((2, n_fft, nq, W), BF16),
            pltpu.VMEM((2, n_fft, nq, W), BF16),
            pltpu.VMEM((2, n_fft, nq, W), BF16),
            pltpu.VMEM((8, cap), F32),
            pltpu.VMEM((nq, cap), BF16),
            pltpu.VMEM((2 * W, cap), BF16),
            pltpu.VMEM((2, NG * PLANES, W), F32),
            pltpu.VMEM((nq, cap), BF16),
            pltpu.VMEM((2, LOW * nq, W), F32),
            pltpu.VMEM((LOW * nq, 2 * W), BF16),
            pltpu.VMEM(((n_fft * W - 1).bit_length(), 8, n_fft * W), jnp.int32),
            pltpu.VMEM(((n_fft * W - 1).bit_length(), 8, n_fft * W), jnp.int32),
            pltpu.VMEM((n_chip, 2, 2, SLOTS, W), BF16),
            pltpu.VMEM(beta.shape, BF16),
            pltpu.VMEM((32 * PAD, W), F32),
            pltpu.VMEM((32, SLOTS * W), BF16),
            pltpu.VMEM((nbr * PAD, W), F32),
            pltpu.VMEM((nbr, SLOTS * W), BF16),
            pltpu.VMEM((32, W), F32),
            pltpu.VMEM((8, W), F32),
            pltpu.VMEM((n_fft, 8, W), F32),
            pltpu.VMEM((nbr * PAD, W), F32),
            pltpu.VMEM((n_chip, 4 * SLOTS, W), BF16),
            pltpu.VMEM((n_chip, 4 * SLOTS, W), BF16),
            pltpu.VMEM(psi.shape, F32),
            dma((2,)), dma((2,)), dma((2,)), dma((2,)),
            dma, dma, dma, dma, dma, dma, dma, dma, dma((len(operands),)), dma((2,)),
        ],
        compiler_params=pltpu.CompilerParams(
            collective_id=0, has_side_effects=True, vmem_limit_bytes=56 * 1024 * 1024
        ),
    )(*operands)


def solution(mesh):
    in_specs = (
        P("band", None, "fft", None),
        P(),
        P(),
        P(),
        P("fft", None),
        P("band", None, None, "fft", None),
        P(),
    )
    out_specs = P("band", None, "fft", None)
    part = functools.partial(body, mesh.shape["band"], mesh.shape["fft"])
    return jax.shard_map(part, mesh=mesh, in_specs=in_specs, out_specs=out_specs, check_vma=False)
```

```python
import functools
import math

import jax
import jax.numpy as jnp
import numpy as np
from jax import lax
from jax.experimental import pallas as pl
from jax.experimental.pallas import tpu as pltpu
from jax.sharding import PartitionSpec as P

NG = 240
RAD = 60
W = 128
SLOTS = 80
PLANES = 8
LOW = 64
PAD = 88
F32 = jnp.float32
BF16 = jnp.bfloat16
MESH = pl.DeviceIdType.MESH


def tables():
    wave = np.arange(W) - RAD
    pos = np.arange(256)
    angle = 2.0 * np.pi * ((wave[:, None] * pos[None, :]) % NG) / NG
    inside = (pos < NG)[None, :]
    co, si = np.cos(angle) * inside, np.sin(angle) * inside
    z_re = np.concatenate([co.T, -si.T], axis=1)
    z_im = np.concatenate([si.T, co.T], axis=1)
    y_out = np.block([[co, si], [-si, co]])
    y_back = y_out.T
    cx, sx = co[:, :NG].T, si[:, :NG].T
    x_out = np.block([[cx, -sx], [sx, cx]])
    x_out = x_out.reshape(2, NG // 16, 16, 2, W).transpose(1, 0, 2, 4, 3).reshape(2 * NG, 2 * W)
    x_back = x_out.T
    return [np.asarray(t, np.float32).astype(jnp.bfloat16) for t in (np.stack([z_re, z_im]), y_out, x_out, x_back, y_back)]


def iota(shape, dim):
    return lax.broadcasted_iota(jnp.int32, shape, dim)


def dot(a, b, dims=((1,), (0,)), precision=None):
    return lax.dot_general(a, b, (dims, ((), ())), preferred_element_type=F32, precision=precision)


NT = ((1,), (1,))
TN = ((0,), (0,))


def kernel(
    n_band, n_fft,
    len_h, col_h, plane_h, col2_h, len2_h, psi_h, pot_h, beta_h, coup_h, zt_h, yf_h, xf_h, xb_h, yb_h,
    out_h,
    len_s, col_s, plane_ref, col_ref, len_ref, psi_ref, pot_ref, beta_ref, coup_ref, zt_ref, yf_ref, xf_ref, xb_ref, yb_ref, out_ref,
    lenb, colb, psi2, z_tab, send1, recv1, send2, recv2,
    chi_f, chi_b, yhot, v3, dense, box, boxes, leave, come,
    gath, beta_other, beta_f, beta_t, psi_f, psi_t, product, part_send, part_recv, term_f, term_send, term_recv, base,
    s1, r1, s2, r2, sg, rg, sp, rp, sn, rn, sb, rb, load_sem, out_sem,
):
    f = lax.axis_index("fft")
    g = lax.axis_index("band")
    nb = 2
    tot = n_fft * SLOTS
    nq = 2 * PLANES
    cap = -(-tot // 2 // W) * W

    def others_along_fft(start):
        n_x = n_fft // 8
        steps = [n_x // 2] + [n_x // 2 + sign * d for d in range(1, n_x // 2 + 1) for sign in (-1, 1) if n_x // 2 + sign * d < n_x]
        x, z = f >> 3, f & 7

        @pl.loop(0, 7)
        def _(j):
            half = (j + 1) >> 1
            to_z = (z + 4 + jnp.where((j & 1) == 1, -half, half)) & 7
            for step in steps:
                start((((x + step) & (n_x - 1)) << 3) + to_z)

        for step in steps:
            if step:
                start((((x + step) & (n_x - 1)) << 3) + z)

    barrier = pltpu.get_barrier_semaphore()

    others_along_fft(lambda e: pl.semaphore_signal(barrier, inc=1, device_id={"fft": e}, device_id_type=MESH))

    n_chip = n_band // 2
    chip = lax.div(g, 2)
    other = g + 1 - 2 * lax.rem(g, 2)

    def same_core(k):
        return lax.rem(g + 2 * k, n_band)

    pl.semaphore_signal(barrier, inc=1, device_id={"band": other}, device_id_type=MESH)
    for k in range(1, n_chip):
        pl.semaphore_signal(barrier, inc=1, device_id={"band": same_core(k)}, device_id_type=MESH)

    pairs = (
        (len_h, len_s), (col_h, col_s), (plane_h, plane_ref), (psi_h, psi_ref), (zt_h, zt_ref), (col2_h, col_ref), (len2_h, len_ref), (pot_h, pot_ref),
        (beta_h, beta_ref), (xf_h, xf_ref), (yf_h, yf_ref), (yb_h, yb_ref), (xb_h, xb_ref), (coup_h, coup_ref),
    )
    loads = [pltpu.make_async_copy(far, near, load_sem.at[i]) for i, (far, near) in enumerate(pairs)]
    for load in loads:
        load.start()
    for load in loads[:5]:
        load.wait()

    @pl.loop(0, SLOTS, unroll=8)
    def _(s):
        lenb[pl.ds(s, 1), :] = jnp.full((1, W), len_s[f * SLOTS + s], jnp.int32)
        colb[pl.ds(s, 1), :] = jnp.full((1, W), col_s[f * SLOTS + s], jnp.int32)

    wave_z = iota((SLOTS, W), 1) - RAD
    in_sphere = (2 * jnp.abs(wave_z) < lenb[...]).astype(F32)
    psi2[...] = jnp.zeros(psi2.shape, BF16)
    for b in range(nb):
        for c in range(2):
            psi2[b, 0:SLOTS, c * W:(c + 1) * W] = (psi_ref[b, c].astype(F32) * in_sphere).astype(BF16)

    n_slot = n_fft * PLANES
    hot_z = (iota((256, n_slot), 0) == plane_ref[...]).astype(F32).T.astype(BF16)
    z_re = dot(hot_z, zt_ref[0]).reshape(n_fft, 1, PLANES, 256)
    z_im = dot(hot_z, zt_ref[1]).reshape(n_fft, 1, PLANES, 256)
    z_tab[...] = jnp.concatenate([z_re, z_im], axis=1).reshape(n_fft * nq, 256).astype(BF16)
    for b in range(nb):
        along = dot(z_tab[...], psi2[b], NT)
        send1[b] = along.reshape(n_fft, nq, W).astype(BF16)
        recv1[b, f] = send1[b, f]

    pl.semaphore_wait(barrier, n_fft - 1 + n_chip)

    def exchange(send, recv, send_sem, recv_sem, b):
        def start(e):
            pltpu.make_async_remote_copy(
                src_ref=send.at[b, e], dst_ref=recv.at[b, f], send_sem=send_sem.at[b], recv_sem=recv_sem.at[b],
                device_id={"fft": e}, device_id_type=MESH,
            ).start()

        others_along_fft(start)

    def wait_bytes(ref, sem):
        pltpu.make_async_copy(ref, ref, sem).wait()

    exchange(send1, recv1, s1, r1, 0)

    def to_chips(k, src, dst, send_sem, recv_sem):
        return pltpu.make_async_remote_copy(
            src_ref=src, dst_ref=dst, send_sem=send_sem, recv_sem=recv_sem,
            device_id={"band": same_core(k)}, device_id_type=MESH,
        )

    for k in range(1, n_chip):
        to_chips(k, psi_ref, gath.at[chip], sg, rg).start()
    loads[8].wait()
    swap_beta = pltpu.make_async_remote_copy(
        src_ref=beta_ref, dst_ref=beta_other, send_sem=sb, recv_sem=rb, device_id={"band": other}, device_id_type=MESH
    )
    swap_beta.start()
    gath[chip] = psi_ref[...]

    def both(mask):
        return jnp.concatenate([mask, mask], axis=0)

    bits = (n_fft * W - 1).bit_length()
    lane8 = iota((8, W), 1)
    lane16 = iota((nq, W), 1).astype(F32).astype(BF16)

    def moved_left(cols, k):
        if k >= 7:
            far = 1 << (k - 7)
            return cols[far:] + [jnp.zeros_like(cols[0])] * min(far, len(cols))
        step = 1 << k
        rolled = [pltpu.roll(col, W - step, 1) for col in cols]
        lane = lane16 if cols[0].dtype == BF16 else lane8
        return [jnp.where(lane < jnp.asarray(W - step, lane.dtype), one, two) for one, two in zip(rolled, rolled[1:] + [jnp.zeros_like(cols[0])])]

    def moved_right(cols, k):
        if k >= 7:
            far = 1 << (k - 7)
            return [jnp.zeros_like(cols[0])] * min(far, len(cols)) + cols[:max(len(cols) - far, 0)]
        step = 1 << k
        rolled = [pltpu.roll(col, step, 1) for col in cols]
        lane = lane16 if cols[0].dtype == BF16 else lane8
        return [jnp.where(lane >= jnp.asarray(step, lane.dtype), one, two) for one, two in zip(rolled, [jnp.zeros_like(cols[0])] + rolled[:-1])]

    def place_tables():
        dense = []
        for r in range(tot // W):
            used = jnp.broadcast_to(len_ref[r:r + 1, :], (8, W)) > 0
            dense.append(jnp.where(used, jnp.broadcast_to(col_ref[r:r + 1, :], (8, W)), -1))
        cols, moves = [], []
        ahead = jnp.zeros((8, 1), F32)
        for e in range(n_fft):
            first, off = 80 * e // W, 80 * e % W
            piece = pltpu.roll(dense[first], W - off, 1) if off else dense[first]
            if off + 80 > W:
                piece = jnp.where(lane8 < W - off, piece, pltpu.roll(dense[first + 1], W - off, 1))
            piece = jnp.where(lane8 < 80, piece, -1)
            used = piece >= 0
            cols.append(piece)
            moves.append(jnp.where(used, jnp.broadcast_to(ahead, (8, W)), 0.0).astype(jnp.int32))
            ahead = ahead + (float(W) - jnp.sum(used.astype(F32), axis=1, keepdims=True))
        for k in range(bits):
            next_moves, next_cols = moved_left(moves, k), moved_left(cols, k)
            for e in range(n_fft):
                leaves, comes = (moves[e] >> k) & 1, (next_moves[e] >> k) & 1
                at = slice(e * W, (e + 1) * W)
                leave[k, :, at] = both(leaves.astype(F32)).astype(BF16)
                come[k, :, at] = both(comes.astype(F32)).astype(BF16)
                moves[e] = jnp.where(comes > 0, next_moves[e], jnp.where(leaves > 0, 0, moves[e]))
                cols[e] = jnp.where(comes > 0, next_cols[e], jnp.where(leaves > 0, -1, cols[e]))
        for r in range(cap // W):
            at = slice(r * W, (r + 1) * W)
            c, d = cols[r] >> 7, cols[r] & (W - 1)
            chi = (c & (LOW - 1)).astype(F32)
            chi_f[:, at] = chi
            chi_b[:, at] = jnp.concatenate([chi, chi], axis=0).astype(BF16)
            row = jnp.where(cols[r] < 0, -1, (c >> 6) * W + d)
            yhot[:, at] = (iota((2 * W, W), 0) == row[:1]).astype(F32).astype(BF16)

    def diagonal():
        gx, gy = colb[...] // W - RAD, colb[...] % W - RAD
        kinetic = (gx * gx + gy * gy + wave_z * wave_z).astype(F32) / float(RAD * RAD)
        for b in range(nb):
            for c in range(2):
                base[b, c] = kinetic * in_sphere * psi_ref[b, c].astype(F32)

    def potential_rows():
        @pl.loop(0, NG // 24)
        def _(m3):
            for u in range(3):
                m = m3 * 3 + u
                for r in range(8):
                    start = 240 * r
                    low = start // W * W
                    width = 256 if start - low <= 16 else 384
                    piece = pot_ref[:, pl.ds(pl.multiple_of(m * 1920 + low, W), width)]
                    if start - low:
                        piece = pltpu.roll(piece, width - (start - low), 1)
                    for c in range(2):
                        v3[c, pl.ds(pl.multiple_of((m * 8 + r) * 8, 8), 8), :] = piece[:, c * W:(c + 1) * W]

    def projector_rows():
        swap_beta.wait_recv()
        for a, source in enumerate((beta_ref, beta_other)):
            for k in range(8):
                for c in range(2):
                    beta_f[pl.ds((c * 16 + a * 8 + k) * PAD, SLOTS), :] = source[0, k, c].astype(F32) * in_sphere

        @pl.loop(0, SLOTS // 4)
        def _(s4):
            for u in range(4):
                s = s4 * 4 + u
                rows = beta_f[pl.ds(s, 32, stride=PAD), :]
                beta_t[:, pl.ds(pl.multiple_of(s * W, W), W)] = rows.astype(BF16)

    def to_planes(b):
        wait_bytes(recv1.at[b, pl.ds(0, n_fft - 1)], r1.at[b])

    def pack_sticks(b):
        cols = [recv1[b, e] for e in range(n_fft)]
        none = jnp.asarray(0, BF16)
        for k in range(bits):
            arriving = moved_left(cols, k)
            cols = [jnp.where(come[k, :, e * W:(e + 1) * W] > none, arriving[e], cols[e]) for e in range(n_fft)]
        dense[...] = jnp.concatenate(cols[:cap // W], axis=1)

    def place_columns(b):
        sticks, place = dense[...], chi_b[...]
        rows = [jnp.where(place == jnp.asarray(i, BF16), sticks, jnp.asarray(0, BF16)) for i in range(LOW)]
        placed = dot(jnp.concatenate(rows, axis=0), yhot[...], NT)
        for h in range(2):
            box[h] = placed[:, h * W:(h + 1) * W]

    def transform():
        @pl.loop(0, PLANES // 4)
        def _(quad):
            along_x = []
            for p in range(2):
                pair = []
                for u in range(2):
                    t = quad * 4 + p * 2 + u
                    pair.append(jnp.concatenate([box[h, pl.ds(t, W, stride=PLANES), :] for h in range(2)], axis=0))
                wide = dot(xf_ref[...], jnp.concatenate(pair, axis=1).astype(BF16)).astype(BF16)
                wide = wide.reshape(NG // 16, 2, 16, 2 * W)
                for u in range(2):
                    part = [wide[:, c, :, u * W:(u + 1) * W].reshape(NG, W) for c in range(2)]
                    along_x.append(jnp.concatenate(part, axis=1))
            full = dot(jnp.concatenate(along_x, axis=0), yf_ref[...])
            weighted = []
            for u in range(4):
                weight = [v3[c, pl.ds(quad * 4 + u, NG, stride=PLANES), :] for c in range(2)]
                weighted.append((full[u * NG:(u + 1) * NG] * jnp.concatenate(weight * 2, axis=1)).astype(BF16))
            back = dot(jnp.concatenate(weighted, axis=0), yb_ref[...]).astype(BF16)
            for p in range(2):
                pair = [back[(p * 2 + u) * NG:(p * 2 + u + 1) * NG] for u in range(2)]
                pair = [part.reshape(NG // 16, 1, 16, 2 * W) for part in pair]
                pair = [jnp.concatenate([part[..., :W], part[..., W:]], axis=1).reshape(2 * NG, W) for part in pair]
                wide = dot(xb_ref[...], jnp.concatenate(pair, axis=1))
                for u in range(2):
                    t = quad * 4 + p * 2 + u
                    for h in range(2):
                        box[h, pl.ds(t, W, stride=PLANES), :] = wide[h * W:(h + 1) * W, u * W:(u + 1) * W]

    def to_sticks(b, beside=None, after=None):
        boxes[...] = jnp.concatenate([box[0], box[1]], axis=1).astype(BF16)

        if beside is not None:
            beside()
        rows = dot(boxes[...], yhot[...])
        place = both(chi_f[...])
        found = jnp.zeros((nq, cap), F32)
        for i in range(LOW):
            found = jnp.where(place == float(i), rows[i * nq:(i + 1) * nq], found)
        none = jnp.asarray(0, BF16)
        cols = [found[:, r * W:(r + 1) * W].astype(BF16) for r in range(cap // W)]
        cols = cols + [jnp.zeros((nq, W), BF16)] * (n_fft - len(cols))
        for k in reversed(range(bits)):
            leaving = moved_right(cols, k)
            cols = [jnp.where(leave[k, :, e * W:(e + 1) * W] > none, leaving[e], cols[e]) for e in range(n_fft)]
        for e in range(n_fft):
            send2[b, e] = cols[e]
        if after is not None:
            after()
        recv2[b, f] = send2[b, f]
        exchange(send2, recv2, s2, r2, b)

    nbr = 2 * nb * n_chip

    def cross(x):
        return jnp.where(iota(x.shape, 1) % 2 == 0, pltpu.roll(x, W - 1, 1), -pltpu.roll(x, 1, 1))

    def psi_rows():
        if n_chip > 1:
            wait_bytes(gath.at[pl.ds(0, n_chip - 1)], rg)
        for h in range(n_chip):
            for b in range(nb):
                for c in range(2):
                    psi_f[pl.ds((h * 4 + b * 2 + c) * PAD, SLOTS), :] = gath[h, b, c].astype(F32)
        for s in range(SLOTS):
            psi_t[:, s * W:(s + 1) * W] = psi_f[pl.ds(s, nbr, stride=PAD), :].astype(BF16)

    def project():
        product[...] = jnp.zeros(product.shape, F32)
        product[:, :nbr] = dot(beta_t[...], psi_t[...], NT)
        one, two = [product[a * 8:a * 8 + 8] + cross(product[16 + a * 8:24 + a * 8]) for a in range(2)]
        part_send[...] = jnp.where(lane8 < nbr, one, pltpu.roll(two, nbr, 1))
        part_recv[f] = part_send[...]

        @pl.loop(1, n_fft)
        def _(k):
            pltpu.make_async_remote_copy(
                src_ref=part_send, dst_ref=part_recv.at[f], send_sem=sp, recv_sem=rp,
                device_id={"fft": lax.rem(f + k, n_fft)}, device_id_type=MESH,
            ).start()

    def term_factors():
        wait_bytes(part_recv.at[pl.ds(0, n_fft - 1)], rp)
        whole = jnp.sum(part_recv[...], axis=0)
        coupling = jnp.concatenate([coup_ref[g], coup_ref[other]], axis=0)
        coupled = dot(coupling, whole, precision=lax.Precision.HIGHEST)
        coeffs = jnp.where(lane8 < nbr, coupled[:8], coupled[8:]).astype(BF16).astype(F32)
        crossed = -cross(coeffs)
        factors = [x if a == 0 else pltpu.roll(x, W - nbr, 1) for x in (coeffs, crossed) for a in range(2)]
        factors = jnp.concatenate(factors + [jnp.zeros((W - 32, W), F32)], axis=0).T[:nbr, :32].astype(BF16)

        return factors

    def expand_rows(factors):
        for m in range(SLOTS // 16):
            terms = dot(factors, beta_t[:, m * 2048:(m + 1) * 2048])
            for i in range(16):
                term_f[pl.ds(m * 16 + i, nbr, stride=PAD), :] = terms[:, i * W:(i + 1) * W]

    def send_terms():
        for k in reversed(range(n_chip)):
            h = lax.div(same_core(k), 2)
            for i in range(4):
                at = pl.ds(pl.multiple_of((h * 4 + i) * PAD, 8), SLOTS)
                term_send[h, i * SLOTS:(i + 1) * SLOTS, :] = term_f[at, :].astype(BF16)
            if k:
                to_chips(k, term_send.at[h], term_recv.at[chip], sn, rn).start()
            else:
                term_recv[chip] = term_send[chip]

    for load in loads[5:8] + loads[9:]:
        load.wait()
    diagonal()
    place_tables()
    exchange(send1, recv1, s1, r1, 1)
    potential_rows()
    projector_rows()
    to_planes(0)
    psi_rows()
    pack_sticks(0)
    place_columns(0)
    project()
    transform()
    to_planes(1)

    def next_band():
        pack_sticks(1)
        place_columns(1)

    to_sticks(0, after=next_band)
    transform()
    factors = term_factors()
    to_sticks(1, lambda: expand_rows(factors))
    send_terms()

    def local_term(b):
        wait_bytes(recv2.at[b, pl.ds(0, n_fft - 1)], r2.at[b])
        local = dot(recv2[b].reshape(n_fft * nq, W), z_tab[...], TN) * (1.0 / float(NG**3))
        return [in_sphere * local[:SLOTS, c * W:(c + 1) * W] for c in range(2)]

    first = local_term(0)
    for c in range(2):
        out_ref[0, c] = base[0, c] + first[c]
    if n_chip > 1:
        wait_bytes(term_recv.at[pl.ds(0, n_chip - 1)], rn)
    stores = [pltpu.make_async_copy(out_ref.at[b], out_h.at[b], out_sem.at[b]) for b in range(nb)]
    for b in range(nb):
        for c in range(2):
            at = pl.ds((b * 2 + c) * SLOTS, SLOTS)
            nonlocal_sum = term_recv[0, at, :].astype(F32)
            for h in range(1, n_chip):
                nonlocal_sum = nonlocal_sum + term_recv[h, at, :].astype(F32)
            if b == 0:
                out_ref[b, c] = out_ref[b, c] + in_sphere * nonlocal_sum
            else:
                base[b, c] = base[b, c] + in_sphere * nonlocal_sum
        if b == 0:
            stores[b].start()
    second = local_term(1)
    for c in range(2):
        out_ref[1, c] = base[1, c] + second[c]
    stores[1].start()

    for b in range(nb):
        wait_bytes(send1.at[b, pl.ds(0, n_fft - 1)], s1.at[b])
        wait_bytes(send2.at[b, pl.ds(0, n_fft - 1)], s2.at[b])
    if n_chip > 1:
        wait_bytes(gath.at[pl.ds(0, n_chip - 1)], sg)
        wait_bytes(term_send.at[pl.ds(0, n_chip - 1)], sn)
    wait_bytes(part_recv.at[pl.ds(0, n_fft - 1)], sp)
    swap_beta.wait_send()
    for b in range(nb):
        stores[b].wait()


def body(n_band, n_fft, psi, stick_col, stick_len, plane_z, potential, beta, coupling):
    tot = n_fft * SLOTS
    n_slot = n_fft * PLANES
    nq = 2 * PLANES
    n_chip = n_band // 2
    nbr = 4 * n_chip
    cap = -(-tot // 2 // W) * W
    consts = [jnp.asarray(t) for t in tables()]
    hbm = pl.BlockSpec(memory_space=pl.ANY)
    dma = pltpu.SemaphoreType.DMA
    operands = [
        stick_len, stick_col, plane_z.reshape(1, n_slot), stick_col.reshape(tot // W, W), stick_len.reshape(tot // W, W),
        psi, potential, beta, coupling, *consts,
    ]
    return pl.pallas_call(
        functools.partial(kernel, n_band, n_fft),
        out_shape=jax.ShapeDtypeStruct(psi.shape, F32),
        in_specs=[hbm] * len(operands),
        out_specs=hbm,
        scratch_shapes=[
            *[(pltpu.SMEM if i < 2 else pltpu.VMEM)(x.shape, x.dtype) for i, x in enumerate(operands)],
            pltpu.VMEM(psi.shape, F32),
            pltpu.VMEM((SLOTS, W), jnp.int32),
            pltpu.VMEM((SLOTS, W), jnp.int32),
            pltpu.VMEM((2, W, 2 * W), BF16),
            pltpu.VMEM((n_fft * nq, 2 * W), BF16),
            pltpu.VMEM((2, n_fft, nq, W), BF16),
            pltpu.VMEM((2, n_fft, nq, W), BF16),
            pltpu.VMEM((2, n_fft, nq, W), BF16),
            pltpu.VMEM((2, n_fft, nq, W), BF16),
            pltpu.VMEM((8, cap), F32),
            pltpu.VMEM((nq, cap), BF16),
            pltpu.VMEM((2 * W, cap), BF16),
            pltpu.VMEM((2, NG * PLANES, W), F32),
            pltpu.VMEM((nq, cap), BF16),
            pltpu.VMEM((2, LOW * nq, W), F32),
            pltpu.VMEM((LOW * nq, 2 * W), BF16),
            pltpu.VMEM(((n_fft * W - 1).bit_length(), nq, n_fft * W), BF16),
            pltpu.VMEM(((n_fft * W - 1).bit_length(), nq, n_fft * W), BF16),
            pltpu.VMEM((n_chip, 2, 2, SLOTS, W), BF16),
            pltpu.VMEM(beta.shape, BF16),
            pltpu.VMEM((32 * PAD, W), F32),
            pltpu.VMEM((32, SLOTS * W), BF16),
            pltpu.VMEM((nbr * PAD, W), F32),
            pltpu.VMEM((nbr, SLOTS * W), BF16),
            pltpu.VMEM((32, W), F32),
            pltpu.VMEM((8, W), F32),
            pltpu.VMEM((n_fft, 8, W), F32),
            pltpu.VMEM((nbr * PAD, W), F32),
            pltpu.VMEM((n_chip, 4 * SLOTS, W), BF16),
            pltpu.VMEM((n_chip, 4 * SLOTS, W), BF16),
            pltpu.VMEM(psi.shape, F32),
            dma((2,)), dma((2,)), dma((2,)), dma((2,)),
            dma, dma, dma, dma, dma, dma, dma, dma, dma((len(operands),)), dma((2,)),
        ],
        compiler_params=pltpu.CompilerParams(
            collective_id=0, has_side_effects=True, vmem_limit_bytes=56 * 1024 * 1024
        ),
    )(*operands)


def solution(mesh):
    in_specs = (
        P("band", None, "fft", None),
        P(),
        P(),
        P(),
        P("fft", None),
        P("band", None, None, "fft", None),
        P(),
    )
    out_specs = P("band", None, "fft", None)
    part = functools.partial(body, mesh.shape["band"], mesh.shape["fft"])
    return jax.shard_map(part, mesh=mesh, in_specs=in_specs, out_specs=out_specs, check_vma=False)
```

```python
import functools
import math

import jax
import jax.numpy as jnp
import numpy as np
from jax import lax
from jax.experimental import pallas as pl
from jax.experimental.pallas import tpu as pltpu
from jax.sharding import PartitionSpec as P

NG = 240
RAD = 60
W = 128
SLOTS = 80
PLANES = 8
LOW = 64
PAD = 88
F32 = jnp.float32
BF16 = jnp.bfloat16
MESH = pl.DeviceIdType.MESH


def tables():
    wave = np.arange(W) - RAD
    pos = np.arange(256)
    angle = 2.0 * np.pi * ((wave[:, None] * pos[None, :]) % NG) / NG
    inside = (pos < NG)[None, :]
    co, si = np.cos(angle) * inside, np.sin(angle) * inside
    z_re = np.concatenate([co.T, -si.T], axis=1)
    z_im = np.concatenate([si.T, co.T], axis=1)
    y_out = np.block([[co, si], [-si, co]])
    y_back = y_out.T
    cx, sx = co[:, :NG].T, si[:, :NG].T
    x_out = np.block([[cx, -sx], [sx, cx]])
    x_out = x_out.reshape(2, NG // 16, 16, 2, W).transpose(1, 0, 2, 4, 3).reshape(2 * NG, 2 * W)
    x_back = x_out.T
    return [np.asarray(t, np.float32).astype(jnp.bfloat16) for t in (np.stack([z_re, z_im]), y_out, x_out, x_back, y_back)]


def iota(shape, dim):
    return lax.broadcasted_iota(jnp.int32, shape, dim)


def dot(a, b, dims=((1,), (0,)), precision=None):
    return lax.dot_general(a, b, (dims, ((), ())), preferred_element_type=F32, precision=precision)


NT = ((1,), (1,))
TN = ((0,), (0,))


def kernel(
    n_band, n_fft,
    len_h, col_h, plane_h, col2_h, len2_h, psi_h, pot_h, beta_h, coup_h, zt_h, yf_h, xf_h, xb_h, yb_h,
    out_h,
    len_s, col_s, plane_ref, col_ref, len_ref, psi_ref, pot_ref, beta_ref, coup_ref, zt_ref, yf_ref, xf_ref, xb_ref, yb_ref, out_ref,
    lenb, colb, psi2, z_tab, send1, recv1, send2, recv2,
    chi_f, chi_b, yhot, v3, dense, box, boxes, leave, come,
    gath, beta_other, beta_f, beta_t, psi_f, psi_t, product, part_send, part_recv, term_f, term_send, term_recv, base,
    s1, r1, s2, r2, sg, rg, sp, rp, sn, rn, sb, rb, load_sem, out_sem,
):
    f = lax.axis_index("fft")
    g = lax.axis_index("band")
    nb = 2
    tot = n_fft * SLOTS
    nq = 2 * PLANES
    cap = -(-tot // 2 // W) * W

    def others_along_fft(start):
        n_x = n_fft // 8
        steps = [n_x // 2] + [n_x // 2 + sign * d for d in range(1, n_x // 2 + 1) for sign in (-1, 1) if n_x // 2 + sign * d < n_x]
        x, z = f >> 3, f & 7

        @pl.loop(0, 7)
        def _(j):
            half = (j + 1) >> 1
            to_z = (z + 4 + jnp.where((j & 1) == 1, -half, half)) & 7
            for step in steps:
                start((((x + step) & (n_x - 1)) << 3) + to_z)

        for step in steps:
            if step:
                start((((x + step) & (n_x - 1)) << 3) + z)

    barrier = pltpu.get_barrier_semaphore()

    others_along_fft(lambda e: pl.semaphore_signal(barrier, inc=1, device_id={"fft": e}, device_id_type=MESH))

    n_chip = n_band // 2
    chip = lax.div(g, 2)
    other = g + 1 - 2 * lax.rem(g, 2)

    by_distance = sorted(range(1, n_chip), key=lambda k: abs(k - n_chip // 2))

    def same_core(k):
        return lax.rem(g + 2 * k, n_band)

    pl.semaphore_signal(barrier, inc=1, device_id={"band": other}, device_id_type=MESH)
    for k in range(1, n_chip):
        pl.semaphore_signal(barrier, inc=1, device_id={"band": same_core(k)}, device_id_type=MESH)

    pairs = (
        (len_h, len_s), (col_h, col_s), (plane_h, plane_ref), (psi_h, psi_ref), (zt_h, zt_ref), (col2_h, col_ref), (len2_h, len_ref), (pot_h, pot_ref),
        (beta_h, beta_ref), (xf_h, xf_ref), (yf_h, yf_ref), (yb_h, yb_ref), (xb_h, xb_ref), (coup_h, coup_ref),
    )
    loads = [pltpu.make_async_copy(far, near, load_sem.at[i]) for i, (far, near) in enumerate(pairs)]
    for load in loads:
        load.start()
    for load in loads[:5]:
        load.wait()

    @pl.loop(0, SLOTS, unroll=8)
    def _(s):
        lenb[pl.ds(s, 1), :] = jnp.full((1, W), len_s[f * SLOTS + s], jnp.int32)
        colb[pl.ds(s, 1), :] = jnp.full((1, W), col_s[f * SLOTS + s], jnp.int32)

    wave_z = iota((SLOTS, W), 1) - RAD
    in_sphere = (2 * jnp.abs(wave_z) < lenb[...]).astype(F32)
    psi2[...] = jnp.zeros(psi2.shape, BF16)
    for b in range(nb):
        for c in range(2):
            psi2[b, 0:SLOTS, c * W:(c + 1) * W] = (psi_ref[b, c].astype(F32) * in_sphere).astype(BF16)

    n_slot = n_fft * PLANES
    hot_z = (iota((256, n_slot), 0) == plane_ref[...]).astype(F32).T.astype(BF16)
    z_re = dot(hot_z, zt_ref[0]).reshape(n_fft, 1, PLANES, 256)
    z_im = dot(hot_z, zt_ref[1]).reshape(n_fft, 1, PLANES, 256)
    z_tab[...] = jnp.concatenate([z_re, z_im], axis=1).reshape(n_fft * nq, 256).astype(BF16)
    for b in range(nb):
        along = dot(z_tab[...], psi2[b], NT)
        send1[b] = along.reshape(n_fft, nq, W).astype(BF16)
        recv1[b, f] = send1[b, f]

    pl.semaphore_wait(barrier, n_fft - 1 + n_chip)

    def exchange(send, recv, send_sem, recv_sem, b):
        def start(e):
            pltpu.make_async_remote_copy(
                src_ref=send.at[b, e], dst_ref=recv.at[b, f], send_sem=send_sem.at[b], recv_sem=recv_sem.at[b],
                device_id={"fft": e}, device_id_type=MESH,
            ).start()

        others_along_fft(start)

    def wait_bytes(ref, sem):
        pltpu.make_async_copy(ref, ref, sem).wait()

    exchange(send1, recv1, s1, r1, 0)

    def to_chips(k, src, dst, send_sem, recv_sem):
        return pltpu.make_async_remote_copy(
            src_ref=src, dst_ref=dst, send_sem=send_sem, recv_sem=recv_sem,
            device_id={"band": same_core(k)}, device_id_type=MESH,
        )

    for k in by_distance:
        to_chips(k, psi_ref, gath.at[chip], sg, rg).start()
    loads[8].wait()
    swap_beta = pltpu.make_async_remote_copy(
        src_ref=beta_ref, dst_ref=beta_other, send_sem=sb, recv_sem=rb, device_id={"band": other}, device_id_type=MESH
    )
    swap_beta.start()
    gath[chip] = psi_ref[...]

    bits = (n_fft * W - 1).bit_length()
    lane8 = iota((8, W), 1)

    def moved_left(cols, k):
        if k >= 7:
            far = 1 << (k - 7)
            return cols[far:] + [jnp.zeros_like(cols[0])] * min(far, len(cols))
        step = 1 << k
        rolled = [pltpu.roll(col, W - step, 1) for col in cols]
        lane = iota(cols[0].shape, 1)
        return [jnp.where(lane < W - step, one, two) for one, two in zip(rolled, rolled[1:] + [jnp.zeros_like(cols[0])])]

    def moved_right(cols, k):
        if k >= 7:
            far = 1 << (k - 7)
            return [jnp.zeros_like(cols[0])] * min(far, len(cols)) + cols[:max(len(cols) - far, 0)]
        step = 1 << k
        rolled = [pltpu.roll(col, step, 1) for col in cols]
        lane = iota(cols[0].shape, 1)
        return [jnp.where(lane >= step, one, two) for one, two in zip(rolled, [jnp.zeros_like(cols[0])] + rolled[:-1])]

    def place_tables():
        dense = []
        for r in range(tot // W):
            used = jnp.broadcast_to(len_ref[r:r + 1, :], (8, W)) > 0
            dense.append(jnp.where(used, jnp.broadcast_to(col_ref[r:r + 1, :], (8, W)), -1))
        cols, moves = [], []
        ahead = jnp.zeros((8, 1), F32)
        for e in range(n_fft):
            first, off = 80 * e // W, 80 * e % W
            piece = pltpu.roll(dense[first], W - off, 1) if off else dense[first]
            if off + 80 > W:
                piece = jnp.where(lane8 < W - off, piece, pltpu.roll(dense[first + 1], W - off, 1))
            piece = jnp.where(lane8 < 80, piece, -1)
            used = piece >= 0
            cols.append(piece)
            moves.append(jnp.where(used, jnp.broadcast_to(ahead, (8, W)), 0.0).astype(jnp.int32))
            ahead = ahead + (float(W) - jnp.sum(used.astype(F32), axis=1, keepdims=True))
        for k in range(bits):
            next_moves, next_cols = moved_left(moves, k), moved_left(cols, k)
            for e in range(n_fft):
                leaves, comes = (moves[e] >> k) & 1, (next_moves[e] >> k) & 1
                at = slice(e * W, (e + 1) * W)
                leave[k, :, at] = leaves
                come[k, :, at] = comes
                moves[e] = jnp.where(comes > 0, next_moves[e], jnp.where(leaves > 0, 0, moves[e]))
                cols[e] = jnp.where(comes > 0, next_cols[e], jnp.where(leaves > 0, -1, cols[e]))
        for r in range(cap // W):
            at = slice(r * W, (r + 1) * W)
            c, d = cols[r] >> 7, cols[r] & (W - 1)
            chi = (c & (LOW - 1)).astype(F32)
            chi_f[:, at] = chi
            chi_b[:, at] = jnp.concatenate([chi, chi], axis=0).astype(BF16)
            row = jnp.where(cols[r] < 0, -1, (c >> 6) * W + d)
            yhot[:, at] = (iota((2 * W, W), 0) == row[:1]).astype(F32).astype(BF16)

    def diagonal():
        gx, gy = colb[...] // W - RAD, colb[...] % W - RAD
        kinetic = (gx * gx + gy * gy + wave_z * wave_z).astype(F32) / float(RAD * RAD)
        for b in range(nb):
            for c in range(2):
                base[b, c] = kinetic * in_sphere * psi_ref[b, c].astype(F32)

    def potential_rows():
        @pl.loop(0, NG // 24)
        def _(m3):
            for u in range(3):
                m = m3 * 3 + u
                for r in range(8):
                    start = 240 * r
                    low = start // W * W
                    width = 256 if start - low <= 16 else 384
                    piece = pot_ref[:, pl.ds(pl.multiple_of(m * 1920 + low, W), width)]
                    if start - low:
                        piece = pltpu.roll(piece, width - (start - low), 1)
                    for c in range(2):
                        v3[c, pl.ds(pl.multiple_of((m * 8 + r) * 8, 8), 8), :] = piece[:, c * W:(c + 1) * W]

    def projector_rows():
        swap_beta.wait_recv()
        for a, source in enumerate((beta_ref, beta_other)):
            for k in range(8):
                for c in range(2):
                    beta_f[pl.ds((c * 16 + a * 8 + k) * PAD, SLOTS), :] = source[0, k, c].astype(F32) * in_sphere

        @pl.loop(0, SLOTS // 4)
        def _(s4):
            for u in range(4):
                s = s4 * 4 + u
                rows = beta_f[pl.ds(s, 32, stride=PAD), :]
                beta_t[:, pl.ds(pl.multiple_of(s * W, W), W)] = rows.astype(BF16)

    def to_planes(b):
        wait_bytes(recv1.at[b, pl.ds(0, n_fft - 1)], r1.at[b])

    def both(mask):
        return jnp.concatenate([mask, mask], axis=0)

    def pack_sticks(b):
        cols = [recv1[b, e].astype(F32) for e in range(n_fft)]
        for k in range(bits):
            arriving = moved_left(cols, k)
            cols = [jnp.where(both(come[k, :, e * W:(e + 1) * W]) > 0, arriving[e], cols[e]) for e in range(n_fft)]
        dense[...] = jnp.concatenate(cols[:cap // W], axis=1).astype(BF16)

    def place_columns(b):
        sticks, place = dense[...], chi_b[...]
        rows = [jnp.where(place == jnp.asarray(i, BF16), sticks, jnp.asarray(0, BF16)) for i in range(LOW)]
        placed = dot(jnp.concatenate(rows, axis=0), yhot[...], NT)
        for h in range(2):
            box[h] = placed[:, h * W:(h + 1) * W]

    def transform():
        @pl.loop(0, PLANES // 4)
        def _(quad):
            along_x = []
            for p in range(2):
                pair = []
                for u in range(2):
                    t = quad * 4 + p * 2 + u
                    pair.append(jnp.concatenate([box[h, pl.ds(t, W, stride=PLANES), :] for h in range(2)], axis=0))
                wide = dot(xf_ref[...], jnp.concatenate(pair, axis=1).astype(BF16)).astype(BF16)
                wide = wide.reshape(NG // 16, 2, 16, 2 * W)
                for u in range(2):
                    part = [wide[:, c, :, u * W:(u + 1) * W].reshape(NG, W) for c in range(2)]
                    along_x.append(jnp.concatenate(part, axis=1))
            full = dot(jnp.concatenate(along_x, axis=0), yf_ref[...])
            weighted = []
            for u in range(4):
                weight = [v3[c, pl.ds(quad * 4 + u, NG, stride=PLANES), :] for c in range(2)]
                weighted.append((full[u * NG:(u + 1) * NG] * jnp.concatenate(weight * 2, axis=1)).astype(BF16))
            back = dot(jnp.concatenate(weighted, axis=0), yb_ref[...]).astype(BF16)
            for p in range(2):
                pair = [back[(p * 2 + u) * NG:(p * 2 + u + 1) * NG] for u in range(2)]
                pair = [part.reshape(NG // 16, 1, 16, 2 * W) for part in pair]
                pair = [jnp.concatenate([part[..., :W], part[..., W:]], axis=1).reshape(2 * NG, W) for part in pair]
                wide = dot(xb_ref[...], jnp.concatenate(pair, axis=1))
                for u in range(2):
                    t = quad * 4 + p * 2 + u
                    for h in range(2):
                        box[h, pl.ds(t, W, stride=PLANES), :] = wide[h * W:(h + 1) * W, u * W:(u + 1) * W]

    def to_sticks(b, beside=None, after=None):
        boxes[...] = jnp.concatenate([box[0], box[1]], axis=1).astype(BF16)

        if beside is not None:
            beside()
        rows = dot(boxes[...], yhot[...])
        place = both(chi_f[...])
        found = jnp.zeros((nq, cap), F32)
        for i in range(LOW):
            found = jnp.where(place == float(i), rows[i * nq:(i + 1) * nq], found)
        cols = [found[:, r * W:(r + 1) * W] for r in range(cap // W)]
        cols = cols + [jnp.zeros((nq, W), F32)] * (n_fft - len(cols))
        for k in reversed(range(bits)):
            leaving = moved_right(cols, k)
            cols = [jnp.where(both(leave[k, :, e * W:(e + 1) * W]) > 0, leaving[e], cols[e]) for e in range(n_fft)]
        for e in range(n_fft):
            send2[b, e] = cols[e].astype(BF16)
        if after is not None:
            after()
        recv2[b, f] = send2[b, f]
        exchange(send2, recv2, s2, r2, b)

    nbr = 2 * nb * n_chip

    def cross(x):
        return jnp.where(iota(x.shape, 1) % 2 == 0, pltpu.roll(x, W - 1, 1), -pltpu.roll(x, 1, 1))

    def psi_rows():
        if n_chip > 1:
            wait_bytes(gath.at[pl.ds(0, n_chip - 1)], rg)
        for h in range(n_chip):
            for b in range(nb):
                for c in range(2):
                    psi_f[pl.ds((h * 4 + b * 2 + c) * PAD, SLOTS), :] = gath[h, b, c].astype(F32)
        for s in range(SLOTS):
            psi_t[:, s * W:(s + 1) * W] = psi_f[pl.ds(s, nbr, stride=PAD), :].astype(BF16)

    def project():
        product[...] = jnp.zeros(product.shape, F32)
        product[:, :nbr] = dot(beta_t[...], psi_t[...], NT)
        one, two = [product[a * 8:a * 8 + 8] + cross(product[16 + a * 8:24 + a * 8]) for a in range(2)]
        part_send[...] = jnp.where(lane8 < nbr, one, pltpu.roll(two, nbr, 1))
        part_recv[f] = part_send[...]

        @pl.loop(1, n_fft)
        def _(k):
            pltpu.make_async_remote_copy(
                src_ref=part_send, dst_ref=part_recv.at[f], send_sem=sp, recv_sem=rp,
                device_id={"fft": lax.rem(f + k, n_fft)}, device_id_type=MESH,
            ).start()

    def term_factors():
        wait_bytes(part_recv.at[pl.ds(0, n_fft - 1)], rp)
        whole = jnp.sum(part_recv[...], axis=0)
        coupling = jnp.concatenate([coup_ref[g], coup_ref[other]], axis=0)
        coupled = dot(coupling, whole, precision=lax.Precision.HIGHEST)
        coeffs = jnp.where(lane8 < nbr, coupled[:8], coupled[8:]).astype(BF16).astype(F32)
        crossed = -cross(coeffs)
        factors = [x if a == 0 else pltpu.roll(x, W - nbr, 1) for x in (coeffs, crossed) for a in range(2)]
        factors = jnp.concatenate(factors + [jnp.zeros((W - 32, W), F32)], axis=0).T[:nbr, :32].astype(BF16)

        return factors

    def expand_rows(factors):
        for m in range(SLOTS // 16):
            terms = dot(factors, beta_t[:, m * 2048:(m + 1) * 2048])
            for i in range(16):
                term_f[pl.ds(m * 16 + i, nbr, stride=PAD), :] = terms[:, i * W:(i + 1) * W]

    def send_terms():
        for k in by_distance + [0]:
            h = lax.div(same_core(k), 2)
            for i in range(4):
                at = pl.ds(pl.multiple_of((h * 4 + i) * PAD, 8), SLOTS)
                term_send[h, i * SLOTS:(i + 1) * SLOTS, :] = term_f[at, :].astype(BF16)
            if k:
                to_chips(k, term_send.at[h], term_recv.at[chip], sn, rn).start()
            else:
                term_recv[chip] = term_send[chip]

    for load in loads[5:8] + loads[9:]:
        load.wait()
    diagonal()
    place_tables()
    exchange(send1, recv1, s1, r1, 1)
    potential_rows()
    projector_rows()
    to_planes(0)
    psi_rows()
    pack_sticks(0)
    place_columns(0)
    project()
    transform()
    to_planes(1)

    def next_band():
        pack_sticks(1)
        place_columns(1)

    to_sticks(0, after=next_band)
    transform()
    factors = term_factors()
    to_sticks(1, lambda: expand_rows(factors))
    send_terms()

    def local_term(b):
        wait_bytes(recv2.at[b, pl.ds(0, n_fft - 1)], r2.at[b])
        local = dot(recv2[b].reshape(n_fft * nq, W), z_tab[...], TN) * (1.0 / float(NG**3))
        return [in_sphere * local[:SLOTS, c * W:(c + 1) * W] for c in range(2)]

    first = local_term(0)
    for c in range(2):
        out_ref[0, c] = base[0, c] + first[c]
    if n_chip > 1:
        wait_bytes(term_recv.at[pl.ds(0, n_chip - 1)], rn)
    stores = [pltpu.make_async_copy(out_ref.at[b], out_h.at[b], out_sem.at[b]) for b in range(nb)]
    for b in range(nb):
        for c in range(2):
            at = pl.ds((b * 2 + c) * SLOTS, SLOTS)
            nonlocal_sum = term_recv[0, at, :].astype(F32)
            for h in range(1, n_chip):
                nonlocal_sum = nonlocal_sum + term_recv[h, at, :].astype(F32)
            if b == 0:
                out_ref[b, c] = out_ref[b, c] + in_sphere * nonlocal_sum
            else:
                base[b, c] = base[b, c] + in_sphere * nonlocal_sum
        if b == 0:
            stores[b].start()
    second = local_term(1)
    for c in range(2):
        out_ref[1, c] = base[1, c] + second[c]
    stores[1].start()

    for b in range(nb):
        wait_bytes(send1.at[b, pl.ds(0, n_fft - 1)], s1.at[b])
        wait_bytes(send2.at[b, pl.ds(0, n_fft - 1)], s2.at[b])
    if n_chip > 1:
        wait_bytes(gath.at[pl.ds(0, n_chip - 1)], sg)
        wait_bytes(term_send.at[pl.ds(0, n_chip - 1)], sn)
    wait_bytes(part_recv.at[pl.ds(0, n_fft - 1)], sp)
    swap_beta.wait_send()
    for b in range(nb):
        stores[b].wait()


def body(n_band, n_fft, psi, stick_col, stick_len, plane_z, potential, beta, coupling):
    tot = n_fft * SLOTS
    n_slot = n_fft * PLANES
    nq = 2 * PLANES
    n_chip = n_band // 2
    nbr = 4 * n_chip
    cap = -(-tot // 2 // W) * W
    consts = [jnp.asarray(t) for t in tables()]
    hbm = pl.BlockSpec(memory_space=pl.ANY)
    dma = pltpu.SemaphoreType.DMA
    operands = [
        stick_len, stick_col, plane_z.reshape(1, n_slot), stick_col.reshape(tot // W, W), stick_len.reshape(tot // W, W),
        psi, potential, beta, coupling, *consts,
    ]
    return pl.pallas_call(
        functools.partial(kernel, n_band, n_fft),
        out_shape=jax.ShapeDtypeStruct(psi.shape, F32),
        in_specs=[hbm] * len(operands),
        out_specs=hbm,
        scratch_shapes=[
            *[(pltpu.SMEM if i < 2 else pltpu.VMEM)(x.shape, x.dtype) for i, x in enumerate(operands)],
            pltpu.VMEM(psi.shape, F32),
            pltpu.VMEM((SLOTS, W), jnp.int32),
            pltpu.VMEM((SLOTS, W), jnp.int32),
            pltpu.VMEM((2, W, 2 * W), BF16),
            pltpu.VMEM((n_fft * nq, 2 * W), BF16),
            pltpu.VMEM((2, n_fft, nq, W), BF16),
            pltpu.VMEM((2, n_fft, nq, W), BF16),
            pltpu.VMEM((2, n_fft, nq, W), BF16),
            pltpu.VMEM((2, n_fft, nq, W), BF16),
            pltpu.VMEM((8, cap), F32),
            pltpu.VMEM((nq, cap), BF16),
            pltpu.VMEM((2 * W, cap), BF16),
            pltpu.VMEM((2, NG * PLANES, W), F32),
            pltpu.VMEM((nq, cap), BF16),
            pltpu.VMEM((2, LOW * nq, W), F32),
            pltpu.VMEM((LOW * nq, 2 * W), BF16),
            pltpu.VMEM(((n_fft * W - 1).bit_length(), 8, n_fft * W), jnp.int32),
            pltpu.VMEM(((n_fft * W - 1).bit_length(), 8, n_fft * W), jnp.int32),
            pltpu.VMEM((n_chip, 2, 2, SLOTS, W), BF16),
            pltpu.VMEM(beta.shape, BF16),
            pltpu.VMEM((32 * PAD, W), F32),
            pltpu.VMEM((32, SLOTS * W), BF16),
            pltpu.VMEM((nbr * PAD, W), F32),
            pltpu.VMEM((nbr, SLOTS * W), BF16),
            pltpu.VMEM((32, W), F32),
            pltpu.VMEM((8, W), F32),
            pltpu.VMEM((n_fft, 8, W), F32),
            pltpu.VMEM((nbr * PAD, W), F32),
            pltpu.VMEM((n_chip, 4 * SLOTS, W), BF16),
            pltpu.VMEM((n_chip, 4 * SLOTS, W), BF16),
            pltpu.VMEM(psi.shape, F32),
            dma((2,)), dma((2,)), dma((2,)), dma((2,)),
            dma, dma, dma, dma, dma, dma, dma, dma, dma((len(operands),)), dma((2,)),
        ],
        compiler_params=pltpu.CompilerParams(
            collective_id=0, has_side_effects=True, vmem_limit_bytes=56 * 1024 * 1024
        ),
    )(*operands)


def solution(mesh):
    in_specs = (
        P("band", None, "fft", None),
        P(),
        P(),
        P(),
        P("fft", None),
        P("band", None, None, "fft", None),
        P(),
    )
    out_specs = P("band", None, "fft", None)
    part = functools.partial(body, mesh.shape["band"], mesh.shape["fft"])
    return jax.shard_map(part, mesh=mesh, in_specs=in_specs, out_specs=out_specs, check_vma=False)
```
